128 devices in a mesh: dp: 4 (over y), ctx: 32 (over z, x, core).
Axes of the slice: x: 4, y: 4, z: 4, core: 2. Of those that a mesh axis runs over, the one named last changes fastest.
Arguments:
- hidden: bfloat16 [4, 4096, 8192], P('dp', 'ctx'), may hold values from -8 to 8
- grad_out: bfloat16 [4, 4096, 2560], P('dp', 'ctx'), may hold values from -8 to 8
- segment: int32 [4, 4096], P('dp', 'ctx'), may hold values from 0 to 31, as said below
Outputs:
- weight_grad: float32 [8192, 2560], P('ctx', 'dp')
The draws below stay inside these ranges and needn't reach their ends.
Inputs may be any that keep to these rules, and one draw needn't show every extreme that they name: `segment`: ids never fall along a row; each of the 32 documents of a row has 1 to 256 tokens; in every row the first and last documents have one token and the second and second-last exactly 256.
All inputs are finite; a program needn't handle non-finite values.
Results may differ from the reference program's by a relative error of at most 0.00074.
Values may be sent and summed in bfloat16 or wider, within the bound.
No kernel may reach another device: no remote copies, remote signals or barrier semaphores. Data moves between devices by JAX's collectives and lax.ppermute only.
A program may use at most 128 MiB of HBM per device.

```python
import math
import jax
import jax.numpy as jnp
from jax import lax

FFW = 8192
DW = 2560
TOK_DEV = 128
ROWS = 4
SEQ = 4096
DOCS = 32
MAXDOC = 256
N_CTX = 32


def copy_links(key):
    subkeys = jax.random.split(key, 2)
    positions = jnp.arange(SEQ, dtype=jnp.int32)
    distance = jax.random.randint(subkeys[0], (ROWS, SEQ), TOK_DEV + 1, 2 * TOK_DEV)
    chosen = jax.random.randint(subkeys[1], (ROWS, SEQ), 0, 8)
    source = (positions[None, :] - distance).astype(jnp.int32)
    linked = jnp.logical_and(chosen > 0, source >= 0)
    source = jnp.where(linked, source, positions[None, :]).astype(jnp.int32)
    anchor = source
    for hop_index in range(SEQ // (TOK_DEV + 1) + 1):
        anchor = jnp.take_along_axis(source, anchor, axis=1).astype(jnp.int32)
    return (linked, anchor)


def mixed_rows(noise, key, linked, anchor, spread, common):
    width = noise.shape[2]
    subkeys = jax.random.split(key, 3)
    log_spread = math.log(spread)
    token_scale = jnp.exp(jax.random.uniform(subkeys[0], (ROWS, SEQ, 1), jnp.float32, -log_spread, log_spread))
    column_scale = jnp.exp(jax.random.uniform(subkeys[1], (ROWS, 1, width), jnp.float32, -log_spread, log_spread))
    base_scale = 0.8 * token_scale * column_scale
    base = base_scale * noise
    copied = jax.vmap(lambda row_base, row_anchor: row_base[row_anchor])(base, anchor)
    values = jnp.where(linked[:, :, None], 0.95 * copied + 0.31 * base, base)
    shared = jax.random.normal(subkeys[2], (ROWS, 1, width), jnp.float32)
    values = values + common * base_scale * shared
    return jnp.clip(values, -8.0, 8.0)


def draw_hidden(key, part):
    linked, anchor = copy_links(key)
    key = jax.random.fold_in(key, 11)
    subkeys = jax.random.split(key, 2)
    noise = jax.random.normal(subkeys[0], (ROWS, SEQ, FFW), jnp.float32)
    spread = 3.1622777
    common = 0.05
    return mixed_rows(noise, subkeys[1], linked, anchor, spread, common).astype(jnp.bfloat16)


def draw_grad_out(key, part):
    linked, anchor = copy_links(key)
    key = jax.random.fold_in(key, 23)
    subkeys = jax.random.split(key, 2)
    noise = jax.random.normal(subkeys[0], (ROWS, SEQ, DW), jnp.float32)
    spread = 3.1622777
    common = 0.05
    return mixed_rows(noise, subkeys[1], linked, anchor, spread, common).astype(jnp.bfloat16)


def draw_segment(key, part):
    key = jax.random.fold_in(key, 37)
    subkeys = jax.random.split(key, 4)
    pair_total = (DOCS - 4) // 2
    first_shift = jax.random.randint(subkeys[0], (ROWS, 1), -(TOK_DEV - 2), TOK_DEV - 1)
    other_size = jax.random.randint(subkeys[1], (ROWS, pair_total - 1), 3 * TOK_DEV // 4, TOK_DEV)
    other_sign = 2 * jax.random.randint(subkeys[3], (ROWS, pair_total - 1), 0, 2) - 1
    other_shift = (other_size * other_sign).astype(jnp.int32)
    middle = jnp.concatenate([TOK_DEV + first_shift - 1, TOK_DEV - first_shift - 1, TOK_DEV + other_shift, TOK_DEV - other_shift], axis=1).astype(jnp.int32)
    row_keys = jax.random.split(subkeys[2], ROWS)
    middle = jax.vmap(lambda row_key, row_lengths: jax.random.permutation(row_key, row_lengths))(row_keys, middle)
    single = jnp.ones((ROWS, 1), jnp.int32)
    longest = jnp.full((ROWS, 1), MAXDOC, jnp.int32)
    lengths = jnp.concatenate([single, longest, middle, longest, single], axis=1).astype(jnp.int32)
    ends = jnp.cumsum(lengths, axis=1).astype(jnp.int32)
    positions = jnp.arange(SEQ, dtype=jnp.int32)
    passed = (positions[None, :, None] >= ends[:, None, :-1]).astype(jnp.int32)
    return jnp.sum(passed, axis=2).astype(jnp.int32)


def setup_inputs(seed: int = 0) -> dict:
    keys = jax.random.split(jax.random.key(seed), 4)
    return {
        "hidden": draw_hidden(jax.random.fold_in(keys[3], 71), 0),
        "grad_out": draw_grad_out(jax.random.fold_in(keys[3], 71), 0),
        "segment": draw_segment(jax.random.fold_in(keys[3], 71), 0),
    }


def pair_terms(own_hidden, own_grad, own_ident, far_hidden, far_grad, far_ident):
    inner_hidden = lax.dot_general(own_hidden, far_hidden, (((1,), (1,)), ((), ())), preferred_element_type=jnp.float32)
    inner_grad = lax.dot_general(own_grad, far_grad, (((1,), (1,)), ((), ())), preferred_element_type=jnp.float32)
    same_doc = own_ident[:, None] == far_ident[None, :]
    return lax.optimization_barrier(jnp.sum(jnp.where(same_doc, inner_hidden * inner_grad, jnp.float32(0.0)), axis=1))

def reference(hidden, grad_out, segment):
    blocks_hidden = hidden.reshape(ROWS, N_CTX, TOK_DEV, FFW)
    blocks_grad = grad_out.reshape(ROWS, N_CTX, TOK_DEV, DW)
    blocks_ident = (segment + 1).reshape(ROWS, N_CTX, TOK_DEV)
    padded_hidden = jnp.concatenate([jnp.zeros((ROWS, 2, TOK_DEV, FFW), hidden.dtype), blocks_hidden], axis=1)
    padded_grad = jnp.concatenate([jnp.zeros((ROWS, 2, TOK_DEV, DW), grad_out.dtype), blocks_grad], axis=1)
    padded_ident = jnp.concatenate([jnp.zeros((ROWS, 2, TOK_DEV), jnp.int32), blocks_ident], axis=1)

    def one_block(flat_index):
        row_index = flat_index // N_CTX
        block_place = flat_index % N_CTX + 2

        def pick_block(offset):
            return (padded_hidden[row_index, block_place - offset], padded_grad[row_index, block_place - offset], padded_ident[row_index, block_place - offset])
        own_block = pick_block(0)
        prior_one = pick_block(1)
        prior_two = pick_block(2)
        pair_sum = pair_terms(*own_block, *own_block)
        pair_sum = pair_sum + 2.0 * pair_terms(*own_block, *prior_one)
        pair_sum = pair_sum + 2.0 * pair_terms(*own_block, *prior_two)
        return pair_sum
    token_terms = lax.map(one_block, jnp.arange(ROWS * N_CTX, dtype=jnp.int32)).reshape(ROWS, SEQ)
    onehot = (segment[:, :, None] == jnp.arange(DOCS, dtype=jnp.int32)[None, None, :]).astype(jnp.float32)
    doc_norms = jnp.einsum('rs,rsd->rd', token_terms, onehot, precision=lax.Precision.HIGHEST)
    clip_bound = math.sqrt(0.5 * MAXDOC * FFW * DW)
    clip_factor = clip_bound / jnp.maximum(jnp.sqrt(doc_norms), clip_bound)
    factor = jnp.einsum('rsd,rd->rs', onehot, clip_factor, precision=lax.Precision.HIGHEST)
    scaled = (grad_out.astype(jnp.float32) * factor[:, :, None] / ROWS).astype(jnp.bfloat16)
    weight_grad = lax.dot_general(hidden.reshape(ROWS * SEQ, FFW), scaled.reshape(ROWS * SEQ, DW), (((0,), (0,)), ((), ())), preferred_element_type=jnp.float32)
    return weight_grad
```

```python
import functools
import math

import jax
import jax.numpy as jnp
from jax import lax
from jax.experimental import pallas as pl
from jax.experimental.pallas import tpu as pltpu
from jax.sharding import PartitionSpec as P

BLK = 128
TILE = 256
DOCS = 32
STEP = 512


def onehot_docs(ids_ref, base, count):
    ids = jnp.concatenate([ids_ref[j] for j in range(count)], axis=1) + base
    docs = lax.broadcasted_iota(jnp.int32, (4 * DOCS, count * BLK), 0)
    return docs == ids


def gram_kernel(parts, finish, rows_ref, ids_ref, *refs):
    h_refs = refs[: sum(parts)]
    g_ref, init_ref, out_ref, h_buf, g_buf, hot_buf, acc = refs[sum(parts) :]
    k = pl.program_id(0)
    i = pl.program_id(1)
    steps = pl.num_programs(1)
    base = rows_ref[k] * DOCS

    @pl.when((k == 0) & (i == 0))
    def _():
        acc[...] = init_ref[...]

    @pl.when(i == 0)
    def _():
        h_buf[1] = jnp.zeros_like(h_buf[1])
        g_buf[1] = jnp.zeros_like(g_buf[1])
        hot_buf[1] = jnp.zeros_like(hot_buf[1])

    slot = lax.rem(i, 2)
    at = 0
    for row, pieces in enumerate(parts):
        span = steps // pieces
        for piece in range(pieces):

            @pl.when((k == row) & (i // span == piece))
            def _(ref=h_refs[at]):
                h_buf[slot] = ref[...].reshape(TILE, ref.shape[2])

            at += 1
    g_buf[slot] = g_ref[...].reshape(TILE, g_ref.shape[2])
    hot = onehot_docs(ids_ref, base, 2)
    hot_buf[slot] = hot.astype(jnp.bfloat16)

    nt = (((1,), (1,)), ((), ()))
    total = jnp.zeros((1, TILE), jnp.float32)
    own_h = h_buf[slot]
    own_g = g_buf[slot]
    own_hot = hot_buf[slot]
    for other in range(2):
        inner_h = lax.dot_general(h_buf[other], own_h, nt, preferred_element_type=jnp.float32)
        inner_g = lax.dot_general(g_buf[other], own_g, nt, preferred_element_type=jnp.float32)
        same = lax.dot_general(
            hot_buf[other], own_hot, (((0,), (0,)), ((), ())), preferred_element_type=jnp.float32
        )
        weight = jnp.where(slot == other, jnp.float32(1.0), jnp.float32(2.0))
        total += weight * jnp.sum(inner_h * inner_g * same, axis=0, keepdims=True)
    terms = jnp.where(hot, jnp.broadcast_to(total, hot.shape), jnp.float32(0.0))
    acc[...] += terms[:, :BLK] + terms[:, BLK:]

    @pl.when((k == pl.num_programs(0) - 1) & (i == steps - 1))
    def _():
        if finish:
            sums = jnp.sum(acc[...].T, axis=0, keepdims=True)
            out_ref[...] = jnp.broadcast_to(sums[None], out_ref.shape)
        else:
            out_ref[...] = acc[...]


def h_specs(parts, blocks, per_step):
    specs = []
    for row, pieces in enumerate(parts):
        span = blocks // per_step // pieces
        for piece in range(pieces):

            def index(k, i, *_, row=row, piece=piece, span=span):
                here = jnp.clip(i - piece * span, 0, span - 1)
                return (jnp.where(k < row, 0, jnp.where(k > row, span - 1, here)), 0, 0)

            specs.append(pl.BlockSpec((per_step, BLK, TILE), index))
    return specs


def gram(rows, ids, parts, pieces, every_grad, init, finish):
    blocks, row_count, _, width = every_grad.shape
    steps = blocks * BLK // TILE
    per_row = steps
    shape = (row_count * blocks, 1, BLK) if finish else (row_count * DOCS, BLK)
    return pl.pallas_call(
        functools.partial(gram_kernel, parts, finish),
        out_shape=jax.ShapeDtypeStruct(shape, jnp.float32),
        grid_spec=pltpu.PrefetchScalarGridSpec(
            num_scalar_prefetch=1,
            grid=(len(parts), steps),
            in_specs=[
                pl.BlockSpec((2, 1, BLK), lambda k, i, r: (r[k] * per_row + i, 0, 0)),
                *h_specs(parts, blocks, 2),
                pl.BlockSpec((2, None, BLK, width), lambda k, i, r: (i, r[k], 0, 0)),
                pl.BlockSpec((row_count * DOCS, BLK), lambda k, i, r: (0, 0)),
            ],
            out_specs=pl.BlockSpec(shape, lambda k, i, r: (0,) * len(shape)),
            scratch_shapes=[
                pltpu.VMEM((2, TILE, TILE), jnp.bfloat16),
                pltpu.VMEM((2, TILE, width), jnp.bfloat16),
                pltpu.VMEM((2, row_count * DOCS, TILE), jnp.bfloat16),
                pltpu.VMEM((row_count * DOCS, BLK), jnp.float32),
            ],
        ),
        compiler_params=pltpu.CompilerParams(vmem_limit_bytes=32 * 2**20),
        cost_estimate=pl.CostEstimate(
            flops=len(parts) * steps * 2 * TILE * TILE * 2 * (TILE + width),
            bytes_accessed=len(parts) * blocks * BLK * 2 * (TILE + width),
            transcendentals=0,
        ),
        name="gram",
    )(rows, ids, *pieces, every_grad, init)


def product_kernel(parts, bound, rows_ref, ids_ref, norms_ref, *refs):
    h_refs = refs[: sum(parts)]
    g_ref, out_ref, clip, scaled = refs[sum(parts) :]
    k = pl.program_id(0)
    i = pl.program_id(1)
    steps = pl.num_programs(1)

    @pl.when((k == 0) & (i == 0))
    def _():
        out_ref[...] = jnp.zeros_like(out_ref)
        norms = jnp.sum(norms_ref[...], axis=0)
        factor = bound / jnp.maximum(jnp.sqrt(norms), bound) / len(parts)
        clip[...] = jnp.broadcast_to(factor, clip.shape).T

    count = STEP // BLK
    hot = onehot_docs(ids_ref, rows_ref[k] * DOCS, count).astype(jnp.float32)
    factor = lax.dot_general(
        hot,
        clip[...],
        (((0,), (0,)), ((), ())),
        precision=lax.Precision.HIGHEST,
        preferred_element_type=jnp.float32,
    )
    width = g_ref.shape[2]
    for j in range(count):
        for c in range(0, width, BLK):
            scaled[j * BLK : (j + 1) * BLK, c : c + BLK] = (
                g_ref[j, :, c : c + BLK].astype(jnp.float32) * factor[j * BLK : (j + 1) * BLK]
            ).astype(jnp.bfloat16)
    at = 0
    for row, pieces in enumerate(parts):
        span = steps // pieces
        for piece in range(pieces):

            @pl.when((k == row) & (i // span == piece))
            def _(ref=h_refs[at]):
                out_ref[...] += lax.dot_general(
                    ref[...].reshape(STEP, ref.shape[2]),
                    scaled[...],
                    (((0,), (0,)), ((), ())),
                    preferred_element_type=jnp.float32,
                )

            at += 1


def product(rows, ids, norms, parts, pieces, every_grad, bound):
    blocks, row_count, _, width = every_grad.shape
    count = STEP // BLK
    steps = blocks // count
    return pl.pallas_call(
        functools.partial(product_kernel, parts, bound),
        out_shape=jax.ShapeDtypeStruct((TILE, width), jnp.float32),
        grid_spec=pltpu.PrefetchScalarGridSpec(
            num_scalar_prefetch=1,
            grid=(len(parts), steps),
            in_specs=[
                pl.BlockSpec((count, 1, BLK), lambda k, i, r: (r[k] * steps + i, 0, 0)),
                pl.BlockSpec(norms.shape, lambda k, i, r: (0, 0, 0)),
                *h_specs(parts, blocks, count),
                pl.BlockSpec((count, None, BLK, width), lambda k, i, r: (i, r[k], 0, 0)),
            ],
            out_specs=pl.BlockSpec((TILE, width), lambda k, i, r: (0, 0)),
            scratch_shapes=[
                pltpu.VMEM((row_count * DOCS, BLK), jnp.float32),
                pltpu.VMEM((STEP, width), jnp.bfloat16),
            ],
        ),
        compiler_params=pltpu.CompilerParams(vmem_limit_bytes=32 * 2**20),
        cost_estimate=pl.CostEstimate(
            flops=2 * row_count * blocks * BLK * TILE * width,
            bytes_accessed=row_count * blocks * BLK * 2 * (TILE + width),
            transcendentals=0,
        ),
        name="product",
    )(rows, ids, norms, *pieces, every_grad)


def shift(block, distance):
    size = lax.axis_size("dp")
    return lax.ppermute(block, "dp", [(i, (i + distance) % size) for i in range(size)])


def body(hidden, grad_out, segment):
    row_count = lax.axis_size("dp")
    blocks = lax.axis_size("ctx")
    tokens, width_hidden = hidden.shape[1:]
    width_grad = grad_out.shape[2]
    me = lax.axis_index("dp")
    rows = lax.rem(me + jnp.array([0, 3, 1, 2], jnp.int32), row_count)

    quarters = grad_out[0].reshape(tokens, row_count, -1).transpose(1, 0, 2)
    quarters = lax.all_to_all(quarters, "dp", 0, 0, tiled=True)
    every_grad = lax.all_gather(quarters, "ctx", axis=0, tiled=False)

    columns = hidden[0].reshape(tokens, blocks, -1).transpose(1, 0, 2)
    own = lax.all_to_all(columns, "ctx", 0, 0, tiled=True)
    below = shift(own, 1)
    above = shift(own, -1)
    far_low = shift(below[: blocks // 2], 1)
    far_high = shift(above[blocks // 2 :], -1)

    ids, own = lax.optimization_barrier((segment, own))
    ids = jnp.broadcast_to(ids[None], (row_count * blocks, 1, tokens))
    ids = lax.all_to_all(ids, ("dp", "ctx"), 0, 0, tiled=True)

    zero = jnp.zeros((row_count * DOCS, tokens), jnp.float32)
    early = gram(rows[:3], ids, (1, 1, 1), (own, below, above), every_grad, zero, False)
    partial = gram(rows[3:], ids, (2,), (far_low, far_high), every_grad, early, True)
    norms = lax.all_to_all(partial, ("dp", "ctx"), 0, 0, tiled=True)

    bound = math.sqrt(tokens * width_hidden * width_grad)
    return product(
        rows,
        ids,
        norms,
        (1, 1, 1, 2),
        (own, below, above, far_low, far_high),
        every_grad,
        bound,
    )


def solution(mesh):
    in_specs = (P("dp", "ctx", None), P("dp", "ctx", None), P("dp", "ctx"))
    out_specs = P("ctx", "dp")
    return jax.shard_map(body, mesh=mesh, in_specs=in_specs, out_specs=out_specs, check_vma=False)
```

```python
import functools
import math

import jax
import jax.numpy as jnp
from jax import lax
from jax.experimental import pallas as pl
from jax.experimental.pallas import tpu as pltpu
from jax.sharding import PartitionSpec as P

BLK = 128
TILE = 256
DOCS = 32
GROUP = 2

NT = (((1,), (1,)), ((), ()))


def flat(ref, at, count):
    return ref[at : at + count].reshape(count * BLK, ref.shape[2])


def gram_kernel(nrows, tiles, finish, rows_ref, ids_ref, first_ref, *refs):
    per_row = 6
    row_refs = [refs[k * per_row : (k + 1) * per_row] for k in range(nrows)]
    init_ref, out_ref, h_prev, g_prev, acc = refs[nrows * per_row :]
    step = pl.program_id(0)
    steps = pl.num_programs(0)

    @pl.when(step == 0)
    def _():
        acc[...] = init_ref[...]
        for k in range(nrows):
            h_last, g_last = row_refs[k][4:]
            h_prev[k, 0] = jnp.zeros_like(h_prev[k, 0])
            g_prev[k, 0] = jnp.zeros_like(g_prev[k, 0])
            h_prev[k, 1] = flat(h_last, 0, 2)
            g_prev[k, 1] = flat(g_last, 0, 2)

    place = lax.broadcasted_iota(jnp.int32, (TILE, TILE), 0)
    column = lax.broadcasted_iota(jnp.int32, (TILE, TILE), 1)
    triangle = jnp.where(
        place < column, jnp.float32(2.0), jnp.where(place == column, jnp.float32(1.0), jnp.float32(0.0))
    )
    docs = lax.broadcasted_iota(jnp.int32, (DOCS, TILE), 0)
    for k in range(nrows):
        base = rows_ref[k]
        share = jnp.zeros((DOCS, BLK), jnp.float32)
        for half in range(2):
            h_ref, g_ref = row_refs[k][2 * half : 2 * half + 2]
            old_h = h_prev[k, half]
            old_g = g_prev[k, half]
            for t in range(tiles):
                number = half * steps * tiles + step * tiles + t
                at = base * (2 * steps * tiles * 2) + 2 * number
                ids = jnp.concatenate([ids_ref[at], ids_ref[at + 1]], axis=1)
                first = jnp.concatenate([first_ref[at], first_ref[at + 1]], axis=1) - number * TILE
                own_h = flat(h_ref, 2 * t, 2)
                own_g = flat(g_ref, 2 * t, 2)
                dot = functools.partial(
                    lax.dot_general, dimension_numbers=NT, preferred_element_type=jnp.float32
                )
                pairs = dot(own_h, own_h) * dot(own_g, own_g) * triangle
                pairs = jnp.where(place >= first, pairs, jnp.float32(0.0))
                far = dot(old_h, own_h) * dot(old_g, own_g)
                far = jnp.where(place >= first + TILE, far, jnp.float32(0.0))
                total = jnp.sum(pairs + 2.0 * far, axis=0, keepdims=True)
                terms = jnp.where(docs == ids, jnp.broadcast_to(total, docs.shape), jnp.float32(0.0))
                share += terms[:, :BLK] + terms[:, BLK:]
                old_h, old_g = own_h, own_g
            h_prev[k, half] = old_h
            g_prev[k, half] = old_g
        here = pl.ds(pl.multiple_of(base * DOCS, DOCS), DOCS)
        acc[here, :] += share

    @pl.when(step == steps - 1)
    def _():
        if finish:
            sums = jnp.sum(acc[...].T, axis=0, keepdims=True)
            out_ref[...] = jnp.broadcast_to(sums[None], out_ref.shape)
        else:
            out_ref[...] = acc[...]


def gram(rows, ids, first, tiles, pieces, init, finish):
    blocks, _, _, width = pieces[0][2].shape
    row_docs = init.shape[0]
    steps = blocks // (4 * tiles)
    shape = (ids.shape[0], 1, BLK) if finish else init.shape
    whole = pl.BlockSpec(ids.shape, lambda i, r: (0, 0, 0))
    specs, operands = [], []
    for h_halves, row, grad in pieces:
        low, high = h_halves
        offset = steps if low is high else 0
        specs += [
            pl.BlockSpec((2 * tiles, BLK, TILE), lambda i, r: (i, 0, 0)),
            pl.BlockSpec((2 * tiles, None, BLK, width), lambda i, r, row=row: (i, row, 0, 0)),
            pl.BlockSpec((2 * tiles, BLK, TILE), lambda i, r, offset=offset: (i + offset, 0, 0)),
            pl.BlockSpec((2 * tiles, None, BLK, width), lambda i, r, row=row: (i + steps, row, 0, 0)),
            pl.BlockSpec((2, BLK, TILE), lambda i, r: (steps * tiles - 1, 0, 0)),
            pl.BlockSpec((2, None, BLK, width), lambda i, r, row=row: (steps * tiles - 1, row, 0, 0)),
        ]
        operands += [low, grad, high, grad, low, grad]
    nrows = len(pieces)
    return pl.pallas_call(
        functools.partial(gram_kernel, nrows, tiles, finish),
        out_shape=jax.ShapeDtypeStruct(shape, jnp.float32),
        grid_spec=pltpu.PrefetchScalarGridSpec(
            num_scalar_prefetch=1,
            grid=(steps,),
            in_specs=[whole, whole, *specs, pl.BlockSpec((row_docs, BLK), lambda i, r: (0, 0))],
            out_specs=pl.BlockSpec(shape, lambda i, r: (0,) * len(shape)),
            scratch_shapes=[
                pltpu.VMEM((nrows, 2, TILE, TILE), jnp.bfloat16),
                pltpu.VMEM((nrows, 2, TILE, width), jnp.bfloat16),
                pltpu.VMEM((row_docs, BLK), jnp.float32),
            ],
        ),
        compiler_params=pltpu.CompilerParams(vmem_limit_bytes=32 * 2**20),
        cost_estimate=pl.CostEstimate(
            flops=nrows * blocks * BLK * 4 * TILE * (TILE + width),
            bytes_accessed=nrows * blocks * BLK * 2 * (TILE + width),
            transcendentals=0,
        ),
        name="gram",
    )(rows, ids, first, *operands, init)


def product_kernel(nrows, bound, rows_ref, ids_ref, norms_ref, *refs):
    per_row = 4
    row_refs = [refs[k * per_row : (k + 1) * per_row] for k in range(nrows)]
    out_ref, factor, turned, scaled = refs[nrows * per_row :]
    step = pl.program_id(0)
    steps = pl.num_programs(0)
    groups = factor.shape[0]
    per_group = groups // nrows

    @pl.when(step == 0)
    def _():
        norms = jnp.sum(norms_ref[...], axis=0)
        clip = bound / jnp.maximum(jnp.sqrt(norms), bound) / nrows
        for k in range(nrows):
            span = slice(k * per_group, (k + 1) * per_group)
            ids = ids_ref[span, 0, :] + k * DOCS
            table = jnp.broadcast_to(clip, ids.shape)
            factor[span, :] = jnp.take_along_axis(table, ids, axis=1)

    lines = []
    for k in range(nrows):
        for half in range(2):
            for j in range(GROUP):
                at = rows_ref[k] * per_group + half * (per_group // 2) + step * GROUP + j
                lines.append(factor[pl.ds(at, 1), :])
    used = len(lines)
    lines = jnp.concatenate(lines + [jnp.zeros((BLK - used, BLK), jnp.float32)], axis=0).T
    at = 0
    for k in range(nrows):
        for half in range(2):
            h_ref, g_ref = row_refs[k][2 * half : 2 * half + 2]
            for j in range(GROUP):
                scale = jnp.broadcast_to(lines[:, at : at + 1], (BLK, BLK))
                here = slice(at * BLK, (at + 1) * BLK)
                for c in range(0, g_ref.shape[2], BLK):
                    scaled[here, c : c + BLK] = (
                        g_ref[j, :, c : c + BLK].astype(jnp.float32) * scale
                    ).astype(jnp.bfloat16)
                turned[:, here] = h_ref[j].T
                at += 1
    result = jnp.dot(turned[...], scaled[...], preferred_element_type=jnp.float32)

    @pl.when(step == 0)
    def _():
        out_ref[...] = result

    @pl.when(step > 0)
    def _():
        out_ref[...] += result


def product(rows, ids, norms, pieces, bound):
    blocks, _, _, width = pieces[0][2].shape
    steps = blocks // (2 * GROUP)
    nrows = len(pieces)
    whole = pl.BlockSpec(ids.shape, lambda i, r: (0, 0, 0))
    specs, operands = [], []
    for h_halves, row, grad in pieces:
        low, high = h_halves
        offset = steps if low is high else 0
        specs += [
            pl.BlockSpec((GROUP, BLK, TILE), lambda i, r: (i, 0, 0)),
            pl.BlockSpec((GROUP, None, BLK, width), lambda i, r, row=row: (i, row, 0, 0)),
            pl.BlockSpec((GROUP, BLK, TILE), lambda i, r, offset=offset: (i + offset, 0, 0)),
            pl.BlockSpec((GROUP, None, BLK, width), lambda i, r, row=row: (i + steps, row, 0, 0)),
        ]
        operands += [low, grad, high, grad]
    depth = nrows * 2 * GROUP * BLK
    return pl.pallas_call(
        functools.partial(product_kernel, nrows, bound),
        out_shape=jax.ShapeDtypeStruct((TILE, width), jnp.float32),
        grid_spec=pltpu.PrefetchScalarGridSpec(
            num_scalar_prefetch=1,
            grid=(steps,),
            in_specs=[whole, whole, *specs],
            out_specs=pl.BlockSpec((TILE, width), lambda i, r: (0, 0)),
            scratch_shapes=[
                pltpu.VMEM((nrows * blocks, BLK), jnp.float32),
                pltpu.VMEM((TILE, depth), jnp.bfloat16),
                pltpu.VMEM((depth, width), jnp.bfloat16),
            ],
        ),
        compiler_params=pltpu.CompilerParams(vmem_limit_bytes=32 * 2**20),
        cost_estimate=pl.CostEstimate(
            flops=2 * nrows * blocks * BLK * TILE * width,
            bytes_accessed=nrows * blocks * BLK * 2 * (TILE + width),
            transcendentals=0,
        ),
        name="product",
    )(rows, ids, norms, *operands)


def shift(block, distance):
    size = lax.axis_size("dp")
    return lax.ppermute(block, "dp", [(i, (i + distance) % size) for i in range(size)])


def starts(ids, row_count):
    by_row = ids.reshape(row_count, -1)
    docs = jnp.arange(DOCS, dtype=jnp.int32)
    before = jnp.sum((by_row[:, None, :] < docs[None, :, None]).astype(jnp.int32), axis=2)
    own = by_row[:, None, :] == docs[None, :, None]
    return jnp.sum(jnp.where(own, before[:, :, None], 0), axis=1).reshape(ids.shape)


def body(hidden, grad_out, segment):
    row_count = lax.axis_size("dp")
    blocks = lax.axis_size("ctx")
    tokens, width_hidden = hidden.shape[1:]
    width_grad = grad_out.shape[2]
    me = lax.axis_index("dp")
    rows = lax.rem(me + jnp.array([0, 3, 1, 2], jnp.int32), row_count)

    quarters = grad_out[0].reshape(tokens, row_count, -1).transpose(1, 0, 2)
    send = lambda d: shift(lax.dynamic_index_in_dim(quarters, lax.rem(me + d + 4, 4), 0, False), d)
    mine = [lax.dynamic_index_in_dim(quarters, me, 0, False), send(1), send(-1), send(2)]
    every_grad = lax.all_gather(jnp.stack(mine), "ctx", axis=0, tiled=False)

    columns = hidden[0].reshape(tokens, blocks, -1).transpose(1, 0, 2)
    own = lax.all_to_all(columns, "ctx", 0, 0, tiled=True)
    below = shift(own, 1)
    above = shift(own, -1)
    far_low = shift(below[: blocks // 2], 1)
    far_high = shift(above[blocks // 2 :], -1)

    ids, own = lax.optimization_barrier((segment, own))
    ids = jnp.broadcast_to(ids[None], (row_count * blocks, 1, tokens))
    ids = lax.all_to_all(ids, ("dp", "ctx"), 0, 0, tiled=True)
    first = starts(ids, row_count)

    pieces = [
        ((own, own), 0, every_grad),
        ((below, below), 1, every_grad),
        ((above, above), 2, every_grad),
        ((far_low, far_high), 3, every_grad),
    ]
    zero = jnp.zeros((row_count * DOCS, tokens), jnp.float32)
    early = gram(rows[:3], ids, first, 1, pieces[:3], zero, False)
    partial = gram(rows[3:], ids, first, 2, pieces[3:], early, True)
    norms = lax.all_to_all(partial, ("dp", "ctx"), 0, 0, tiled=True)

    bound = math.sqrt(tokens * width_hidden * width_grad)
    return product(rows, ids, norms, pieces, bound)


def solution(mesh):
    in_specs = (P("dp", "ctx", None), P("dp", "ctx", None), P("dp", "ctx"))
    out_specs = P("ctx", "dp")
    return jax.shard_map(body, mesh=mesh, in_specs=in_specs, out_specs=out_specs, check_vma=False)
```

```python
import functools
import math

import jax
import jax.numpy as jnp
from jax import lax
from jax.experimental import pallas as pl
from jax.experimental.pallas import tpu as pltpu
from jax.sharding import PartitionSpec as P

BLK = 128
TILE = 256
DOCS = 32
GROUP = 4

NT = (((1,), (1,)), ((), ()))


def flat(ref, at, count):
    return ref[at : at + count].reshape(count * BLK, ref.shape[2])


def flat_pair(refs, at, count):
    return jnp.concatenate([flat(ref, at, count) for ref in refs], axis=1)


def gram_kernel(nrows, tiles, rows_ref, ids_ref, first_ref, *refs):
    per_row = 9
    row_refs = [refs[k * per_row : (k + 1) * per_row] for k in range(nrows)]
    out_ref, h_prev, g_prev, acc = refs[nrows * per_row :]
    step = pl.program_id(0)
    steps = pl.num_programs(0)

    @pl.when(step == 0)
    def _():
        acc[...] = jnp.zeros_like(acc)
        for k in range(nrows):
            g_last = row_refs[k][8]
            h_prev[k, 0] = jnp.zeros_like(h_prev[k, 0])
            g_prev[k, 0] = jnp.zeros_like(g_prev[k, 0])
            h_prev[k, 1] = flat_pair(row_refs[k][6:8], 0, 2)
            g_prev[k, 1] = flat(g_last, 0, 2)

    place = lax.broadcasted_iota(jnp.int32, (TILE, TILE), 0)
    column = lax.broadcasted_iota(jnp.int32, (TILE, TILE), 1)
    triangle = jnp.where(
        place < column, jnp.float32(2.0), jnp.where(place == column, jnp.float32(1.0), jnp.float32(0.0))
    )
    docs = lax.broadcasted_iota(jnp.int32, (DOCS, TILE), 0)
    for k in range(nrows):
        base = rows_ref[k]
        share = jnp.zeros((DOCS, BLK), jnp.float32)
        for half in range(2):
            h_refs = row_refs[k][3 * half : 3 * half + 2]
            g_ref = row_refs[k][3 * half + 2]
            old_h = h_prev[k, half]
            old_g = g_prev[k, half]
            for t in range(tiles):
                number = half * steps * tiles + step * tiles + t
                at = base * (2 * steps * tiles * 2) + 2 * number
                ids = jnp.concatenate([ids_ref[at], ids_ref[at + 1]], axis=1)
                first = jnp.concatenate([first_ref[at], first_ref[at + 1]], axis=1) - number * TILE
                own_h = flat_pair(h_refs, 2 * t, 2)
                own_g = flat(g_ref, 2 * t, 2)
                dot = functools.partial(
                    lax.dot_general, dimension_numbers=NT, preferred_element_type=jnp.float32
                )
                pairs = dot(own_h, own_h) * dot(own_g, own_g) * triangle
                pairs = jnp.where(place >= first, pairs, jnp.float32(0.0))
                far = dot(old_h, own_h) * dot(old_g, own_g)
                far = jnp.where(place >= first + TILE, far, jnp.float32(0.0))
                total = jnp.sum(pairs + 2.0 * far, axis=0, keepdims=True)
                terms = jnp.where(docs == ids, jnp.broadcast_to(total, docs.shape), jnp.float32(0.0))
                share += terms[:, :BLK] + terms[:, BLK:]
                old_h, old_g = own_h, own_g
            h_prev[k, half] = old_h
            g_prev[k, half] = old_g
        here = pl.ds(pl.multiple_of(base * DOCS, DOCS), DOCS)
        acc[here, :] += share

    @pl.when(step == steps - 1)
    def _():
        sums = jnp.sum(acc[...].T, axis=0, keepdims=True)
        out_ref[...] = jnp.broadcast_to(sums[None], out_ref.shape)


def row_specs(count, steps, width, row):
    specs = []
    for offset in (0, steps):
        for _ in range(2):
            specs.append(pl.BlockSpec((count, BLK, BLK), lambda i, r, o=offset: (i + o, 0, 0)))
        specs.append(
            pl.BlockSpec((count, None, BLK, width), lambda i, r, o=offset: (i + o, row, 0, 0))
        )
    return specs


def gram(rows, ids, first, tiles, pieces):
    blocks, _, _, width = pieces[0][3].shape
    steps = blocks // (4 * tiles)
    shape = (ids.shape[0], 1, BLK)
    whole = pl.BlockSpec(ids.shape, lambda i, r: (0, 0, 0))
    last = steps * tiles - 1
    specs, operands = [], []
    for left, right, row, grad in pieces:
        specs += row_specs(2 * tiles, steps, width, row)
        specs += [pl.BlockSpec((2, BLK, BLK), lambda i, r: (last, 0, 0))] * 2
        specs += [pl.BlockSpec((2, None, BLK, width), lambda i, r, row=row: (last, row, 0, 0))]
        operands += [left, right, grad] * 3
    nrows = len(pieces)
    return pl.pallas_call(
        functools.partial(gram_kernel, nrows, tiles),
        out_shape=jax.ShapeDtypeStruct(shape, jnp.float32),
        grid_spec=pltpu.PrefetchScalarGridSpec(
            num_scalar_prefetch=1,
            grid=(steps,),
            in_specs=[whole, whole, *specs],
            out_specs=pl.BlockSpec(shape, lambda i, r: (0, 0, 0)),
            scratch_shapes=[
                pltpu.VMEM((nrows, 2, TILE, TILE), jnp.bfloat16),
                pltpu.VMEM((nrows, 2, TILE, width), jnp.bfloat16),
                pltpu.VMEM((nrows * DOCS, BLK), jnp.float32),
            ],
        ),
        compiler_params=pltpu.CompilerParams(vmem_limit_bytes=32 * 2**20),
        cost_estimate=pl.CostEstimate(
            flops=nrows * blocks * BLK * 4 * TILE * (TILE + width),
            bytes_accessed=nrows * blocks * BLK * 2 * (TILE + width),
            transcendentals=0,
        ),
        name="gram",
    )(rows, ids, first, *operands)


def product_kernel(nrows, bound, rows_ref, ids_ref, norms_ref, *refs):
    per_row = 6
    row_refs = [refs[k * per_row : (k + 1) * per_row] for k in range(nrows)]
    out_ref, factor, scaled = refs[nrows * per_row :]
    step = pl.program_id(0)
    steps = pl.num_programs(0)
    groups = factor.shape[0]
    per_group = groups // nrows

    @pl.when(step == 0)
    def _():
        norms = jnp.sum(norms_ref[...], axis=0)
        clip = bound / jnp.maximum(jnp.sqrt(norms), bound) / nrows
        for k in range(nrows):
            span = slice(k * per_group, (k + 1) * per_group)
            ids = ids_ref[span, 0, :] + k * DOCS
            table = jnp.broadcast_to(clip, ids.shape)
            factor[span, :] = jnp.take_along_axis(table, ids, axis=1)

    lines = []
    for k in range(nrows):
        for half in range(2):
            for j in range(GROUP):
                at = rows_ref[k] * per_group + half * (per_group // 2) + step * GROUP + j
                lines.append(factor[pl.ds(at, 1), :])
    used = len(lines)
    lines = jnp.concatenate(lines + [jnp.zeros((BLK - used, BLK), jnp.float32)], axis=0).T
    at = 0
    result = None
    for k in range(nrows):
        for half in range(2):
            h_refs = row_refs[k][3 * half : 3 * half + 2]
            g_ref = row_refs[k][3 * half + 2]
            begin = at * BLK
            for j in range(GROUP):
                scale = jnp.broadcast_to(lines[:, at : at + 1], (BLK, BLK))
                here = slice(at * BLK, (at + 1) * BLK)
                for c in range(0, g_ref.shape[2], BLK):
                    scaled[here, c : c + BLK] = (
                        g_ref[j, :, c : c + BLK].astype(jnp.float32) * scale
                    ).astype(jnp.bfloat16)
                at += 1
            share = lax.dot_general(
                flat_pair(h_refs, 0, GROUP),
                scaled[begin : at * BLK, :],
                (((0,), (0,)), ((), ())),
                preferred_element_type=jnp.float32,
            )
            result = share if result is None else result + share

    @pl.when(step == 0)
    def _():
        out_ref[...] = result

    @pl.when(step > 0)
    def _():
        out_ref[...] += result


def product(rows, ids, norms, pieces, bound):
    blocks, _, _, width = pieces[0][3].shape
    steps = blocks // (2 * GROUP)
    nrows = len(pieces)
    whole = pl.BlockSpec(ids.shape, lambda i, r: (0, 0, 0))
    specs, operands = [], []
    for left, right, row, grad in pieces:
        specs += row_specs(GROUP, steps, width, row)
        operands += [left, right, grad] * 2
    return pl.pallas_call(
        functools.partial(product_kernel, nrows, bound),
        out_shape=jax.ShapeDtypeStruct((TILE, width), jnp.float32),
        grid_spec=pltpu.PrefetchScalarGridSpec(
            num_scalar_prefetch=1,
            grid=(steps,),
            in_specs=[whole, whole, *specs],
            out_specs=pl.BlockSpec((TILE, width), lambda i, r: (0, 0)),
            scratch_shapes=[
                pltpu.VMEM((nrows * blocks, BLK), jnp.float32),
                pltpu.VMEM((nrows * 2 * GROUP * BLK, width), jnp.bfloat16),
            ],
        ),
        compiler_params=pltpu.CompilerParams(vmem_limit_bytes=32 * 2**20),
        cost_estimate=pl.CostEstimate(
            flops=2 * nrows * blocks * BLK * TILE * width,
            bytes_accessed=nrows * blocks * BLK * 2 * (TILE + width),
            transcendentals=0,
        ),
        name="product",
    )(rows, ids, norms, *operands)


def quarters_kernel(rows_ref, *refs):
    ins, outs = refs[: len(refs) // 2], refs[len(refs) // 2 :]
    for in_ref, out_ref in zip(ins, outs):
        out_ref[...] = in_ref[...]


def quarters(targets, grad):
    tokens, width = grad.shape
    count = targets.shape[0]
    part = width // count
    return pl.pallas_call(
        quarters_kernel,
        out_shape=[jax.ShapeDtypeStruct((tokens, part), grad.dtype)] * count,
        grid_spec=pltpu.PrefetchScalarGridSpec(
            num_scalar_prefetch=1,
            grid=(1,),
            in_specs=[pl.BlockSpec((tokens, part), lambda i, r, k=k: (0, r[k])) for k in range(count)],
            out_specs=[pl.BlockSpec((tokens, part), lambda i, r: (0, 0))] * count,
        ),
        name="quarters",
    )(targets, *[grad] * count)


def columns_kernel(in_ref, left_ref, right_ref):
    for j in range(left_ref.shape[0]):
        left_ref[j] = in_ref[:, 2 * j * BLK : (2 * j + 1) * BLK]
        right_ref[j] = in_ref[:, (2 * j + 1) * BLK : (2 * j + 2) * BLK]


def columns(hidden, blocks, steps=4):
    tokens, width = hidden.shape
    count = blocks // steps
    half = pl.BlockSpec((count, tokens, BLK), lambda i: (i, 0, 0))
    return pl.pallas_call(
        columns_kernel,
        out_shape=[jax.ShapeDtypeStruct((blocks, tokens, BLK), hidden.dtype)] * 2,
        grid=(steps,),
        in_specs=[pl.BlockSpec((tokens, width // steps), lambda i: (0, i))],
        out_specs=[half, half],
        name="columns",
    )(hidden)


def shift(block, distance):
    size = lax.axis_size("dp")
    return lax.ppermute(block, "dp", [(i, (i + distance) % size) for i in range(size)])


def starts(ids, row_count):
    by_row = ids.reshape(row_count, -1)
    docs = jnp.arange(DOCS, dtype=jnp.int32)
    before = jnp.sum((by_row[:, None, :] < docs[None, :, None]).astype(jnp.int32), axis=2)
    own = by_row[:, None, :] == docs[None, :, None]
    return jnp.sum(jnp.where(own, before[:, :, None], 0), axis=1).reshape(ids.shape)


def body(hidden, grad_out, segment):
    row_count = lax.axis_size("dp")
    blocks = lax.axis_size("ctx")
    tokens, width_hidden = hidden.shape[1:]
    width_grad = grad_out.shape[2]
    me = lax.axis_index("dp")
    rows = lax.rem(me + jnp.array([0, 3, 1, 2], jnp.int32), row_count)

    keep, up, down, across = quarters(lax.rem(me + jnp.array([0, 1, 3, 2], jnp.int32), row_count), grad_out[0])
    received = [keep, shift(up, 1), shift(down, -1), shift(across, 2)]

    left, right = columns(hidden[0], blocks)
    left, right, *received = lax.optimization_barrier((left, right, *received))

    every_grad = lax.all_gather(jnp.stack(received), "ctx", axis=0, tiled=False)

    left = lax.all_to_all(left, "ctx", 0, 0, tiled=True)
    left_below, left_above = shift(left, 1), shift(left, -1)
    right, left_ready = lax.optimization_barrier((right, left))
    right = lax.all_to_all(right, "ctx", 0, 0, tiled=True)
    right_below, right_above = shift(right, 1), shift(right, -1)
    left_far = shift(left_below, 1)
    right_far = shift(right_above, -1)

    ids, right_ready = lax.optimization_barrier((segment, right))
    ids = jnp.broadcast_to(ids[None], (row_count * blocks, 1, tokens))
    ids = lax.all_to_all(ids, ("dp", "ctx"), 0, 0, tiled=True)
    first = starts(ids, row_count)

    pieces = [
        (left, right, 0, every_grad),
        (left_below, right_below, 1, every_grad),
        (left_above, right_above, 2, every_grad),
        (left_far, right_far, 3, every_grad),
    ]
    partial = gram(rows, ids, first, 1, pieces)
    norms = lax.all_to_all(partial, ("dp", "ctx"), 0, 0, tiled=True)

    bound = math.sqrt(tokens * width_hidden * width_grad)
    return product(rows, ids, norms, pieces, bound)


def solution(mesh):
    in_specs = (P("dp", "ctx", None), P("dp", "ctx", None), P("dp", "ctx"))
    out_specs = P("ctx", "dp")
    return jax.shard_map(body, mesh=mesh, in_specs=in_specs, out_specs=out_specs, check_vma=False)
```

```python
import functools
import math

import jax
import jax.numpy as jnp
from jax import lax
from jax.experimental import pallas as pl
from jax.experimental.pallas import tpu as pltpu
from jax.sharding import PartitionSpec as P

BLK = 128
TILE = 256
DOCS = 32
GROUP = 2

NT = (((1,), (1,)), ((), ()))


def flat(ref, at, count):
    return ref[at : at + count].reshape(count * BLK, ref.shape[2])


def flat_pair(refs, at, count):
    return jnp.concatenate([flat(ref, at, count) for ref in refs], axis=1)


def gram_kernel(kinds, tiles, finish, rows_ref, ids_ref, first_ref, *refs):
    per_row = 9
    nrows = len(kinds)
    row_refs = [refs[k * per_row : (k + 1) * per_row] for k in range(nrows)]
    init_ref, out_ref, h_prev, g_prev, acc = refs[nrows * per_row :]
    step = pl.program_id(0)
    steps = pl.num_programs(0)

    @pl.when(step == 0)
    def _():
        acc[...] = init_ref[...]
        for k in range(nrows):
            h_prev[k, 0] = jnp.zeros_like(h_prev[k, 0])
            g_prev[k, 0] = jnp.zeros_like(g_prev[k, 0])
            h_prev[k, 1] = flat_pair(row_refs[k][6:8], 0, 2)
            g_prev[k, 1] = flat(row_refs[k][8], 0, 2)

    place = lax.broadcasted_iota(jnp.int32, (TILE, TILE), 0)
    column = lax.broadcasted_iota(jnp.int32, (TILE, TILE), 1)
    triangle = jnp.where(
        place < column, jnp.float32(2.0), jnp.where(place == column, jnp.float32(1.0), jnp.float32(0.0))
    )
    docs = lax.broadcasted_iota(jnp.int32, (DOCS, TILE), 0)
    dot = functools.partial(lax.dot_general, dimension_numbers=NT, preferred_element_type=jnp.float32)
    for k, row in enumerate(kinds):
        share = jnp.zeros((DOCS, BLK), jnp.float32)
        line = slice(row, row + 1)
        for half in range(2):
            h_refs = row_refs[k][3 * half : 3 * half + 2]
            g_ref = row_refs[k][3 * half + 2]
            old_h = h_prev[k, half]
            old_g = g_prev[k, half]
            for t in range(tiles):
                number = half * steps * tiles + step * tiles + t
                at = 2 * number
                ids = jnp.concatenate([ids_ref[at, line], ids_ref[at + 1, line]], axis=1)
                first = jnp.concatenate([first_ref[at, line], first_ref[at + 1, line]], axis=1)
                first = first - number * TILE
                own_h = flat_pair(h_refs, 2 * t, 2)
                own_g = flat(g_ref, 2 * t, 2)
                pairs = dot(own_h, own_h) * dot(own_g, own_g) * triangle
                pairs = jnp.where(place >= first, pairs, jnp.float32(0.0))
                far = dot(old_h, own_h) * dot(old_g, own_g)
                far = jnp.where(place >= first + TILE, far, jnp.float32(0.0))
                total = jnp.sum(pairs + 2.0 * far, axis=0, keepdims=True)
                terms = jnp.where(docs == ids, jnp.broadcast_to(total, docs.shape), jnp.float32(0.0))
                share += terms[:, :BLK] + terms[:, BLK:]
                old_h, old_g = own_h, own_g
            h_prev[k, half] = old_h
            g_prev[k, half] = old_g
        here = pl.ds(pl.multiple_of(rows_ref[row] * DOCS, DOCS), DOCS)
        acc[here, :] += share

    @pl.when(step == steps - 1)
    def _():
        if finish:
            sums = jnp.sum(acc[...].T, axis=0, keepdims=True)
            out_ref[...] = jnp.broadcast_to(sums[None], out_ref.shape)
        else:
            out_ref[...] = acc[...]


def row_specs(count, steps, width, row):
    specs = []
    for offset in (0, steps):
        for _ in range(2):
            specs.append(pl.BlockSpec((count, BLK, BLK), lambda i, r, o=offset: (i + o, 0, 0)))
        specs.append(
            pl.BlockSpec((count, None, BLK, width), lambda i, r, o=offset: (i + o, row, 0, 0))
        )
    return specs


def gram(rows, ids, first, tiles, pieces, init, devices):
    blocks, _, _, width = pieces[0][3].shape
    steps = blocks // (4 * tiles)
    shape = (devices, 1, BLK) if devices else init.shape
    whole = pl.BlockSpec(ids.shape, lambda i, r: (0, 0, 0))
    last = steps * tiles - 1
    specs, operands = [], []
    for left, right, _, grad, place in pieces:
        specs += row_specs(2 * tiles, steps, width, place)
        specs += [pl.BlockSpec((2, BLK, BLK), lambda i, r: (last, 0, 0))] * 2
        specs += [pl.BlockSpec((2, None, BLK, width), lambda i, r, p=place: (last, p, 0, 0))]
        operands += [left, right, grad] * 3
    nrows = len(pieces)
    return pl.pallas_call(
        functools.partial(gram_kernel, [piece[2] for piece in pieces], tiles, bool(devices)),
        out_shape=jax.ShapeDtypeStruct(shape, jnp.float32),
        grid_spec=pltpu.PrefetchScalarGridSpec(
            num_scalar_prefetch=1,
            grid=(steps,),
            in_specs=[whole, whole, *specs, pl.BlockSpec(init.shape, lambda i, r: (0, 0))],
            out_specs=pl.BlockSpec(shape, lambda i, r: (0,) * len(shape)),
            scratch_shapes=[
                pltpu.VMEM((nrows, 2, TILE, TILE), jnp.bfloat16),
                pltpu.VMEM((nrows, 2, TILE, width), jnp.bfloat16),
                pltpu.VMEM(init.shape, jnp.float32),
            ],
        ),
        compiler_params=pltpu.CompilerParams(vmem_limit_bytes=50 * 2**20),
        cost_estimate=pl.CostEstimate(
            flops=nrows * blocks * BLK * 4 * TILE * (TILE + width),
            bytes_accessed=nrows * blocks * BLK * 2 * (TILE + width),
            transcendentals=0,
        ),
        name="gram",
    )(rows, ids, first, *operands, init)


def product_kernel(nrows, bound, rows_ref, ids_ref, norms_ref, *refs):
    per_row = 6
    row_refs = [refs[k * per_row : (k + 1) * per_row] for k in range(nrows)]
    out_ref, factor, scaled = refs[nrows * per_row :]
    step = pl.program_id(0)
    steps = pl.num_programs(0)
    blocks = ids_ref.shape[0]

    @pl.when(step == 0)
    def _():
        norms = jnp.sum(norms_ref[...], axis=0)
        clip = bound / jnp.maximum(jnp.sqrt(norms), bound) / nrows
        for k in range(nrows):
            ids = ids_ref[:, k, :] + rows_ref[k] * DOCS
            table = jnp.broadcast_to(clip, ids.shape)
            factor[k] = jnp.take_along_axis(table, ids, axis=1)

    lines = []
    for k in range(nrows):
        for half in range(2):
            for j in range(GROUP):
                at = half * (blocks // 2) + step * GROUP + j
                lines.append(factor[k, pl.ds(at, 1), :])
    used = len(lines)
    lines = jnp.concatenate(lines + [jnp.zeros((BLK - used, BLK), jnp.float32)], axis=0).T
    at = 0
    result = None
    for k in range(nrows):
        for half in range(2):
            h_refs = row_refs[k][3 * half : 3 * half + 2]
            g_ref = row_refs[k][3 * half + 2]
            begin = at * BLK
            for j in range(GROUP):
                scale = jnp.broadcast_to(lines[:, at : at + 1], (BLK, BLK))
                here = slice(at * BLK, (at + 1) * BLK)
                for c in range(0, g_ref.shape[2], BLK):
                    scaled[here, c : c + BLK] = (
                        g_ref[j, :, c : c + BLK].astype(jnp.float32) * scale
                    ).astype(jnp.bfloat16)
                at += 1
            share = lax.dot_general(
                flat_pair(h_refs, 0, GROUP),
                scaled[begin : at * BLK, :],
                (((0,), (0,)), ((), ())),
                preferred_element_type=jnp.float32,
            )
            result = share if result is None else result + share

    @pl.when(step == 0)
    def _():
        out_ref[...] = result

    @pl.when(step > 0)
    def _():
        out_ref[...] += result


def product(rows, ids, norms, pieces, bound):
    blocks, _, _, width = pieces[0][3].shape
    steps = blocks // (2 * GROUP)
    nrows = len(pieces)
    whole = pl.BlockSpec(ids.shape, lambda i, r: (0, 0, 0))
    specs, operands = [], []
    for left, right, _, grad, place in pieces:
        specs += row_specs(GROUP, steps, width, place)
        operands += [left, right, grad] * 2
    return pl.pallas_call(
        functools.partial(product_kernel, nrows, bound),
        out_shape=jax.ShapeDtypeStruct((TILE, width), jnp.float32),
        grid_spec=pltpu.PrefetchScalarGridSpec(
            num_scalar_prefetch=1,
            grid=(steps,),
            in_specs=[whole, pl.BlockSpec(norms.shape, lambda i, r: (0, 0, 0)), *specs],
            out_specs=pl.BlockSpec((TILE, width), lambda i, r: (0, 0)),
            scratch_shapes=[
                pltpu.VMEM((nrows, blocks, BLK), jnp.float32),
                pltpu.VMEM((nrows * 2 * GROUP * BLK, width), jnp.bfloat16),
            ],
        ),
        compiler_params=pltpu.CompilerParams(vmem_limit_bytes=24 * 2**20),
        cost_estimate=pl.CostEstimate(
            flops=2 * nrows * blocks * BLK * TILE * width,
            bytes_accessed=nrows * blocks * BLK * 2 * (TILE + width),
            transcendentals=0,
        ),
        name="product",
    )(rows, ids, norms, *operands)


def quarters_kernel(me_ref, ids_ref, *refs):
    ins, outs = refs[: len(refs) // 2], refs[len(refs) // 2 :]
    tokens = ins[0].shape[0]
    for in_ref, out_ref in zip(ins, outs):
        out_ref[:tokens, :] = in_ref[...]
        ids = ids_ref[...].astype(jnp.float32).astype(jnp.bfloat16)
        out_ref[tokens:, :BLK] = jnp.broadcast_to(ids, (16, BLK))
        out_ref[tokens:, BLK:] = jnp.zeros((16, out_ref.shape[1] - BLK), jnp.bfloat16)


def quarters(me, offsets, grad, ids):
    tokens, width = grad.shape
    count = len(offsets)
    part = width // count
    return pl.pallas_call(
        quarters_kernel,
        out_shape=[jax.ShapeDtypeStruct((tokens + 16, part), grad.dtype)] * count,
        grid_spec=pltpu.PrefetchScalarGridSpec(
            num_scalar_prefetch=1,
            grid=(1,),
            in_specs=[pl.BlockSpec(ids.shape, lambda i, m: (0, 0))]
            + [
                pl.BlockSpec((tokens, part), lambda i, m, o=o: (0, lax.rem(m[0] + o, count)))
                for o in offsets
            ],
            out_specs=[pl.BlockSpec((tokens + 16, part), lambda i, m: (0, 0))] * count,
        ),
        name="quarters",
    )(me, ids, *[grad] * count)


def columns_kernel(in_ref, left_ref, right_ref):
    for j in range(left_ref.shape[0]):
        left_ref[j] = in_ref[:, 2 * j * BLK : (2 * j + 1) * BLK]
        right_ref[j] = in_ref[:, (2 * j + 1) * BLK : (2 * j + 2) * BLK]


def columns(hidden, blocks, steps=4):
    tokens, width = hidden.shape
    count = blocks // steps
    half = pl.BlockSpec((count, tokens, BLK), lambda i: (i, 0, 0))
    return pl.pallas_call(
        columns_kernel,
        out_shape=[jax.ShapeDtypeStruct((blocks, tokens, BLK), hidden.dtype)] * 2,
        grid=(steps,),
        in_specs=[pl.BlockSpec((tokens, width // steps), lambda i: (0, i))],
        out_specs=[half, half],
        name="columns",
    )(hidden)


def shift(block, distance):
    size = lax.axis_size("dp")
    return lax.ppermute(block, "dp", [(i, (i + distance) % size) for i in range(size)])


def starts(ids):
    docs = jnp.arange(DOCS, dtype=jnp.int32)
    before = jnp.sum((ids[None] < docs[:, None, None, None]).astype(jnp.int32), axis=(1, 3))
    own = ids[None] == docs[:, None, None, None]
    return jnp.sum(jnp.where(own, before[:, None, :, None], 0), axis=0)


def body(hidden, grad_out, segment):
    row_count = lax.axis_size("dp")
    blocks = lax.axis_size("ctx")
    tokens, width_hidden = hidden.shape[1:]
    width_grad = grad_out.shape[2]
    me = lax.axis_index("dp")

    keep, up, down, across = quarters(me[None], (0, 1, 3, 2), grad_out[0], segment)
    received = [keep, shift(up, 1), shift(down, -1), shift(across, 2)]

    left, right = columns(hidden[0], blocks)
    left, right, *received = lax.optimization_barrier((left, right, *received))

    grads = jnp.stack([part[:tokens] for part in received])
    every_grad = lax.all_gather(grads, "ctx", axis=0, tiled=False)

    left = lax.all_to_all(left, "ctx", 0, 0, tiled=True)
    left_below, left_above = lax.optimization_barrier((shift(left, 1), shift(left, -1)))
    right, left_ready = lax.optimization_barrier((right, left))
    right = lax.all_to_all(right, "ctx", 0, 0, tiled=True)
    right_below, right_above = lax.optimization_barrier((shift(right, 1), shift(right, -1)))
    left_far = shift(left_below, 1)
    right_far = shift(right_above, -1)

    ids = jnp.stack([part[tokens, :BLK] for part in received]).astype(jnp.int32)
    ids, right_ready = lax.optimization_barrier((ids, right))
    ids = jnp.broadcast_to(ids[None], (blocks, row_count, tokens))
    ids = lax.all_to_all(ids, "ctx", 0, 0, tiled=True)
    first = starts(ids)

    rows = lax.rem(me + jnp.array([0, 3, 1, 2], jnp.int32), row_count)
    pieces = [
        (left, right, 0, every_grad, 0),
        (left_below, right_below, 1, every_grad, 1),
        (left_above, right_above, 2, every_grad, 2),
        (left_far, right_far, 3, every_grad, 3),
    ]
    zero = jnp.zeros((row_count * DOCS, BLK), jnp.float32)
    early = gram(rows, ids, first, 1, pieces[:3], zero, 0)
    partial = gram(rows, ids, first, 2, pieces[3:], early, row_count * blocks)
    norms = lax.all_to_all(partial, ("dp", "ctx"), 0, 0, tiled=True)

    bound = math.sqrt(tokens * width_hidden * width_grad)
    return product(rows, ids, norms, pieces, bound)


def solution(mesh):
    in_specs = (P("dp", "ctx", None), P("dp", "ctx", None), P("dp", "ctx"))
    out_specs = P("ctx", "dp")
    return jax.shard_map(body, mesh=mesh, in_specs=in_specs, out_specs=out_specs, check_vma=False)
```

```python
import functools
import math

import jax
import jax.numpy as jnp
from jax import lax
from jax.experimental import pallas as pl
from jax.experimental.pallas import tpu as pltpu
from jax.sharding import PartitionSpec as P

BLK = 128
TILE = 256
DOCS = 32
GROUP = 4

NT = (((1,), (1,)), ((), ()))
TN = (((0,), (0,)), ((), ()))


def flat(block):
    return block.reshape(block.shape[0] * block.shape[1], block.shape[2])


def columns_of(refs, at, count):
    return jnp.concatenate([flat(ref[pl.ds(at, count)]) for ref in refs], axis=1)


def gram_kernel(kinds, tiles, finish, rows_ref, ids_ref, first_ref, *refs):
    nrows = len(kinds)
    h_refs = [refs[2 * k : 2 * k + 2] for k in range(nrows)]
    g_ref, init_ref, out_ref, g_prev, acc = refs[2 * nrows :]
    step = pl.program_id(0)

    @pl.when(step == 0)
    def _():
        acc[...] = init_ref[...]
        g_prev[...] = jnp.zeros_like(g_prev)

    place = lax.broadcasted_iota(jnp.int32, (TILE, TILE), 0)
    column = lax.broadcasted_iota(jnp.int32, (TILE, TILE), 1)
    triangle = jnp.where(
        place < column, jnp.float32(2.0), jnp.where(place == column, jnp.float32(1.0), jnp.float32(0.0))
    )
    docs = lax.broadcasted_iota(jnp.int32, (DOCS, TILE), 0)
    dot = functools.partial(lax.dot_general, dimension_numbers=NT, preferred_element_type=jnp.float32)
    for k, row in enumerate(kinds):
        share = jnp.zeros((DOCS, BLK), jnp.float32)
        line = slice(row, row + 1)
        old_h = columns_of(h_refs[k], jnp.maximum(2 * step * tiles - 2, 0), 2)
        old_g = g_prev[k]
        for t in range(tiles):
            number = step * tiles + t
            at = 2 * number
            ids = jnp.concatenate([ids_ref[at, line], ids_ref[at + 1, line]], axis=1)
            first = jnp.concatenate([first_ref[at, line], first_ref[at + 1, line]], axis=1)
            first = first - number * TILE
            own_h = columns_of(h_refs[k], at, 2)
            own_g = flat(g_ref[2 * t : 2 * t + 2, k])
            pairs = dot(own_h, own_h) * dot(own_g, own_g) * triangle
            pairs = jnp.where(place >= first, pairs, jnp.float32(0.0))
            far = dot(old_h, own_h) * dot(old_g, own_g)
            far = jnp.where(place >= first + TILE, far, jnp.float32(0.0))
            total = jnp.sum(pairs + 2.0 * far, axis=0, keepdims=True)
            terms = jnp.where(docs == ids, jnp.broadcast_to(total, docs.shape), jnp.float32(0.0))
            share += terms[:, :BLK] + terms[:, BLK:]
            old_h, old_g = own_h, own_g
        g_prev[k] = old_g
        here = pl.ds(pl.multiple_of(rows_ref[row] * DOCS, DOCS), DOCS)
        acc[here, :] += share

    @pl.when(step == pl.num_programs(0) - 1)
    def _():
        if finish:
            sums = jnp.sum(acc[...].T, axis=0, keepdims=True)
            out_ref[...] = jnp.broadcast_to(sums[None], out_ref.shape)
        else:
            out_ref[...] = acc[...]


def gram(rows, ids, first, tiles, kinds, hidden, grad, init, devices):
    blocks, _, _, width = grad.shape
    nrows = len(kinds)
    count = 2 * tiles
    shape = (devices, 1, BLK) if devices else init.shape
    whole = pl.BlockSpec(ids.shape, lambda i, r: (0, 0, 0))
    place = kinds[0] // nrows
    return pl.pallas_call(
        functools.partial(gram_kernel, kinds, tiles, bool(devices)),
        out_shape=jax.ShapeDtypeStruct(shape, jnp.float32),
        grid_spec=pltpu.PrefetchScalarGridSpec(
            num_scalar_prefetch=1,
            grid=(blocks // count,),
            in_specs=[
                whole,
                whole,
                *[pl.BlockSpec(memory_space=pltpu.VMEM)] * (2 * nrows),
                pl.BlockSpec((count, nrows, BLK, width), lambda i, r: (i, place, 0, 0)),
                pl.BlockSpec(init.shape, lambda i, r: (0, 0)),
            ],
            out_specs=pl.BlockSpec(shape, lambda i, r: (0,) * len(shape)),
            scratch_shapes=[
                pltpu.VMEM((nrows, TILE, width), jnp.bfloat16),
                pltpu.VMEM(init.shape, jnp.float32),
            ],
        ),
        compiler_params=pltpu.CompilerParams(vmem_limit_bytes=40 * 2**20),
        cost_estimate=pl.CostEstimate(
            flops=nrows * blocks * BLK * 4 * TILE * (TILE + width),
            bytes_accessed=nrows * blocks * BLK * 2 * (TILE + width),
            transcendentals=0,
        ),
        name="gram",
    )(rows, ids, first, *[half for pair in hidden for half in pair], grad, init)


def product_kernel(nrows, bound, rows_ref, ids_ref, norms_ref, *refs):
    h_refs = [refs[2 * k : 2 * k + 2] for k in range(nrows)]
    g_ref, out_ref, factor, scaled = refs[2 * nrows :]
    step = pl.program_id(0)

    @pl.when(step == 0)
    def _():
        norms = jnp.sum(norms_ref[...], axis=0)
        clip = bound / jnp.maximum(jnp.sqrt(norms), bound) / nrows
        for k in range(nrows):
            ids = ids_ref[:, k, :] + rows_ref[k] * DOCS
            table = jnp.broadcast_to(clip, ids.shape)
            factor[k] = jnp.take_along_axis(table, ids, axis=1)

    lines = [factor[k, pl.ds(step * GROUP + j, 1), :] for k in range(nrows) for j in range(GROUP)]
    used = len(lines)
    lines = jnp.concatenate(lines + [jnp.zeros((BLK - used, BLK), jnp.float32)], axis=0).T
    result = None
    for k in range(nrows):
        for j in range(GROUP):
            at = k * GROUP + j
            scale = jnp.broadcast_to(lines[:, at : at + 1], (BLK, BLK))
            for c in range(0, g_ref.shape[3], BLK):
                scaled[at * BLK : (at + 1) * BLK, c : c + BLK] = (
                    g_ref[j, k, :, c : c + BLK].astype(jnp.float32) * scale
                ).astype(jnp.bfloat16)
        share = lax.dot_general(
            columns_of(h_refs[k], step * GROUP, GROUP),
            scaled[k * GROUP * BLK : (k + 1) * GROUP * BLK, :],
            TN,
            preferred_element_type=jnp.float32,
        )
        result = share if result is None else result + share

    @pl.when(step == 0)
    def _():
        out_ref[...] = result

    @pl.when(step > 0)
    def _():
        out_ref[...] += result


def product(rows, ids, norms, hidden, grad, bound):
    blocks, nrows, _, width = grad.shape
    return pl.pallas_call(
        functools.partial(product_kernel, nrows, bound),
        out_shape=jax.ShapeDtypeStruct((TILE, width), jnp.float32),
        grid_spec=pltpu.PrefetchScalarGridSpec(
            num_scalar_prefetch=1,
            grid=(blocks // GROUP,),
            in_specs=[
                pl.BlockSpec(ids.shape, lambda i, r: (0, 0, 0)),
                pl.BlockSpec(norms.shape, lambda i, r: (0, 0, 0)),
                *[pl.BlockSpec(memory_space=pltpu.VMEM)] * (2 * nrows),
                pl.BlockSpec((GROUP, nrows, BLK, width), lambda i, r: (i, 0, 0, 0)),
            ],
            out_specs=pl.BlockSpec((TILE, width), lambda i, r: (0, 0)),
            scratch_shapes=[
                pltpu.VMEM((nrows, blocks, BLK), jnp.float32),
                pltpu.VMEM((nrows * GROUP * BLK, width), jnp.bfloat16),
            ],
        ),
        compiler_params=pltpu.CompilerParams(vmem_limit_bytes=40 * 2**20),
        cost_estimate=pl.CostEstimate(
            flops=2 * nrows * blocks * BLK * TILE * width,
            bytes_accessed=nrows * blocks * BLK * 2 * (TILE + width),
            transcendentals=0,
        ),
        name="product",
    )(rows, ids, norms, *[half for pair in hidden for half in pair], grad)


def quarters_kernel(me_ref, ids_ref, *refs):
    ins, outs = refs[: len(refs) // 2], refs[len(refs) // 2 :]
    tokens = ins[0].shape[0]
    for in_ref, out_ref in zip(ins, outs):
        out_ref[:tokens, :] = in_ref[...]
        ids = ids_ref[...].astype(jnp.float32).astype(jnp.bfloat16)
        out_ref[tokens:, :BLK] = jnp.broadcast_to(ids, (16, BLK))
        out_ref[tokens:, BLK:] = jnp.zeros((16, out_ref.shape[1] - BLK), jnp.bfloat16)


def quarters(me, offsets, grad, ids):
    tokens, width = grad.shape
    count = len(offsets)
    part = width // count
    return pl.pallas_call(
        quarters_kernel,
        out_shape=[jax.ShapeDtypeStruct((tokens + 16, part), grad.dtype)] * count,
        grid_spec=pltpu.PrefetchScalarGridSpec(
            num_scalar_prefetch=1,
            grid=(1,),
            in_specs=[pl.BlockSpec(ids.shape, lambda i, m: (0, 0))]
            + [
                pl.BlockSpec((tokens, part), lambda i, m, o=o: (0, lax.rem(m[0] + o, count)))
                for o in offsets
            ],
            out_specs=[pl.BlockSpec((tokens + 16, part), lambda i, m: (0, 0))] * count,
        ),
        name="quarters",
    )(me, ids, *[grad] * count)


def columns_kernel(in_ref, left_ref, right_ref):
    for j in range(left_ref.shape[0]):
        left_ref[j] = in_ref[:, 2 * j * BLK : (2 * j + 1) * BLK]
        right_ref[j] = in_ref[:, (2 * j + 1) * BLK : (2 * j + 2) * BLK]


def columns(hidden, blocks, steps=4):
    tokens, width = hidden.shape
    count = blocks // steps
    half = pl.BlockSpec((count, tokens, BLK), lambda i: (i, 0, 0))
    return pl.pallas_call(
        columns_kernel,
        out_shape=[jax.ShapeDtypeStruct((blocks, tokens, BLK), hidden.dtype)] * 2,
        grid=(steps,),
        in_specs=[pl.BlockSpec((tokens, width // steps), lambda i: (0, i))],
        out_specs=[half, half],
        name="columns",
    )(hidden)


def shift(block, distance):
    size = lax.axis_size("dp")
    return lax.ppermute(block, "dp", [(i, (i + distance) % size) for i in range(size)])


def starts(ids):
    docs = jnp.arange(DOCS, dtype=jnp.int32)
    before = jnp.sum((ids[None] < docs[:, None, None, None]).astype(jnp.int32), axis=(1, 3))
    own = ids[None] == docs[:, None, None, None]
    return jnp.sum(jnp.where(own, before[:, None, :, None], 0), axis=0)


def body(hidden, grad_out, segment):
    row_count = lax.axis_size("dp")
    blocks = lax.axis_size("ctx")
    tokens, width_hidden = hidden.shape[1:]
    width_grad = grad_out.shape[2]
    me = lax.axis_index("dp")

    keep, up, down, across = quarters(me[None], (0, 1, 3, 2), grad_out[0], segment)
    received = [keep, shift(up, 1), shift(down, -1), shift(across, 2)]

    left, right = columns(hidden[0], blocks)
    left, right, *received = lax.optimization_barrier((left, right, *received))

    grads = jnp.stack([part[:tokens] for part in received])
    every_grad = lax.all_gather(grads, "ctx", axis=0, tiled=False)

    left = lax.all_to_all(left, "ctx", 0, 0, tiled=True)
    left_below, left_above = lax.optimization_barrier((shift(left, 1), shift(left, -1)))
    right, left_ready = lax.optimization_barrier((right, left))
    right = lax.all_to_all(right, "ctx", 0, 0, tiled=True)
    right_below, right_above = lax.optimization_barrier((shift(right, 1), shift(right, -1)))
    left_far = shift(left_below, 1)
    right_far = shift(right_above, -1)

    ids = jnp.stack([part[tokens, :BLK] for part in received]).astype(jnp.int32)
    ids, right_ready = lax.optimization_barrier((ids, right))
    ids = jnp.broadcast_to(ids[None], (blocks, row_count, tokens))
    ids = lax.all_to_all(ids, "ctx", 0, 0, tiled=True)
    first = starts(ids)

    rows = lax.rem(me + jnp.array([0, 3, 1, 2], jnp.int32), row_count)
    pairs = [
        (left, right),
        (left_below, right_below),
        (left_above, right_above),
        (left_far, right_far),
    ]
    zero = jnp.zeros((row_count * DOCS, BLK), jnp.float32)
    early = gram(rows, ids, first, 2, (0, 1, 2), pairs[:3], every_grad, zero, 0)
    partial = gram(rows, ids, first, 4, (3,), pairs[3:], every_grad, early, row_count * blocks)
    norms = lax.all_to_all(partial, ("dp", "ctx"), 0, 0, tiled=True)

    bound = math.sqrt(tokens * width_hidden * width_grad)
    return product(rows, ids, norms, pairs, every_grad, bound)


def solution(mesh):
    in_specs = (P("dp", "ctx", None), P("dp", "ctx", None), P("dp", "ctx"))
    out_specs = P("ctx", "dp")
    return jax.shard_map(body, mesh=mesh, in_specs=in_specs, out_specs=out_specs, check_vma=False)
```

```python
import functools
import math

import jax
import jax.numpy as jnp
from jax import lax
from jax.experimental import pallas as pl
from jax.experimental.pallas import tpu as pltpu
from jax.sharding import PartitionSpec as P

BLK = 128
TILE = 256
DOCS = 32
DEPTH = 8
HALVES = 2
PARTS = 4
AHEAD = 3

NT = (((1,), (1,)), ((), ()))
TN = (((0,), (0,)), ((), ()))


def flat(block):
    return block.reshape(block.shape[0] * block.shape[1], block.shape[2])


def columns_of(refs, at, count):
    return jnp.concatenate([flat(ref[pl.ds(at, count)]) for ref in refs], axis=1)


def gram_dot(left, right):
    return lax.dot_general(left, right, NT, preferred_element_type=jnp.float32)


def places():
    spot = lax.broadcasted_iota(jnp.int32, (TILE, TILE), 0)
    column = lax.broadcasted_iota(jnp.int32, (TILE, TILE), 1)
    return spot, column


def pair_products(old, own):
    spot, column = places()
    return jnp.where(spot <= column, gram_dot(own, own), gram_dot(old, own))


def counted(pairs, first):
    spot, column = places()
    weight = jnp.where(spot == column, jnp.float32(1.0), jnp.float32(2.0))
    begin = jnp.where(spot <= column, first, first + TILE)
    return jnp.where(spot >= begin, pairs * weight, jnp.float32(0.0))


def line_of(ref, at, row):
    line = slice(row, row + 1)
    return jnp.concatenate([ref[at, line], ref[at + 1, line]], axis=1)


def doc_sums(terms, ids):
    docs = lax.broadcasted_iota(jnp.int32, (DOCS, TILE), 0)
    total = jnp.sum(terms, axis=0, keepdims=True)
    parts = jnp.where(docs == ids, jnp.broadcast_to(total, docs.shape), jnp.float32(0.0))
    return parts[:, :BLK] + parts[:, BLK:]


def hidden_kernel(kinds, first_ref, *refs):
    nrows = len(kinds)
    per_row = 2 * HALVES
    out_ref = refs[per_row * nrows]
    tiles = out_ref.shape[1]
    step = pl.program_id(0)
    for k, row in enumerate(kinds):
        row_refs = refs[per_row * k : per_row * (k + 1)]
        old = columns_of(row_refs[HALVES:], 0, 2)
        for t in range(tiles):
            number = step * tiles + t
            first = line_of(first_ref, 2 * number, row) - number * TILE
            own = columns_of(row_refs[:HALVES], 2 * t, 2)
            out_ref[k, t] = counted(pair_products(old, own), first)
            old = own


def hidden_gram(first, kinds, hidden):
    pieces = [piece for row in hidden for piece in row]
    blocks = pieces[0].shape[0]
    count = blocks // PARTS
    tiles = count // 2
    nrows = len(kinds)
    own = pl.BlockSpec((count, BLK, BLK), lambda i: (i, 0, 0))
    old = pl.BlockSpec((2, BLK, BLK), lambda i: (jnp.maximum(i * tiles - 1, 0), 0, 0))
    return pl.pallas_call(
        functools.partial(hidden_kernel, kinds),
        out_shape=pltpu.HBM((nrows, blocks // 2, TILE, TILE), jnp.float32),
        grid=(PARTS,),
        in_specs=[
            pl.BlockSpec(first.shape, lambda i: (0, 0, 0)),
            *[spec for _ in kinds for spec in [own] * HALVES + [old] * HALVES],
        ],
        out_specs=pl.BlockSpec((nrows, tiles, TILE, TILE), lambda i: (0, i, 0, 0)),
        compiler_params=pltpu.CompilerParams(vmem_limit_bytes=24 * 2**20),
        cost_estimate=pl.CostEstimate(
            flops=nrows * blocks * BLK * 4 * TILE * TILE,
            bytes_accessed=nrows * blocks * BLK * TILE * 6,
            transcendentals=0,
        ),
        name="hidden_gram",
    )(first, *[piece for row in hidden for piece in [*row, *row]])


def early_kernel(kinds, rows_ref, ids_ref, pairs_hbm, g_hbm, out_ref, g_ref, pairs_ref, pair_sems, sems):
    nrows = len(kinds)
    blocks, every = g_ref.shape[:2]
    count = blocks // PARTS
    tiles = count // 2

    def copy(n):
        here = pl.ds(lax.rem(n, PARTS) * count, count)
        row = n // PARTS
        return pltpu.make_async_copy(g_hbm.at[here, row], g_ref.at[here, row], sems.at[n])

    def pair_copy(n):
        here = pl.ds(lax.rem(n, PARTS) * tiles, tiles)
        slot = lax.rem(n, AHEAD + 1)
        return pltpu.make_async_copy(pairs_hbm.at[n // PARTS, here], pairs_ref.at[slot], pair_sems.at[n])

    for n in range(AHEAD):
        copy(n).start()
        pair_copy(n).start()
    out_ref[...] = jnp.zeros_like(out_ref)
    for k, row in enumerate(kinds):

        @pl.loop(0, PARTS)
        def _(c, k=k, row=row):
            n = k * PARTS + c
            copy(n).wait()
            pair_copy(n).wait()

            @pl.when(n + AHEAD < every * PARTS)
            def _():
                copy(n + AHEAD).start()

            @pl.when(n + AHEAD < nrows * PARTS)
            def _():
                pair_copy(n + AHEAD).start()

            slot = lax.rem(n, AHEAD + 1)
            share = jnp.zeros((DOCS, BLK), jnp.float32)
            old = flat(g_ref[pl.ds(jnp.maximum(c * count - 2, 0), 2), row])
            for t in range(tiles):
                at = c * count + 2 * t
                own = flat(g_ref[pl.ds(at, 2), row])
                terms = pairs_ref[slot, t] * pair_products(old, own)
                share += doc_sums(terms, line_of(ids_ref, at, row))
                old = own
            here = pl.ds(pl.multiple_of(rows_ref[row] * DOCS, DOCS), DOCS)
            out_ref[here, :] += share

    for n in range(nrows * PARTS, every * PARTS):
        copy(n).wait()
        if n + AHEAD < every * PARTS:
            copy(n + AHEAD).start()


def late_kernel(row, rows_ref, ids_ref, first_ref, *refs):
    h_refs = refs[:HALVES]
    g_ref, init_ref, out_ref, acc = refs[HALVES:]
    count = g_ref.shape[0] // PARTS
    acc[...] = init_ref[...]

    @pl.loop(0, PARTS)
    def _(c):
        share = jnp.zeros((DOCS, BLK), jnp.float32)
        before = jnp.maximum(c * count - 2, 0)
        old_h = columns_of(h_refs, before, 2)
        old_g = flat(g_ref[pl.ds(before, 2), row])
        for t in range(count // 2):
            at = c * count + 2 * t
            first = line_of(first_ref, at, row) - at * BLK
            own_h = columns_of(h_refs, at, 2)
            own_g = flat(g_ref[pl.ds(at, 2), row])
            terms = counted(pair_products(old_h, own_h) * pair_products(old_g, own_g), first)
            share += doc_sums(terms, line_of(ids_ref, at, row))
            old_h, old_g = own_h, own_g
        here = pl.ds(pl.multiple_of(rows_ref[row] * DOCS, DOCS), DOCS)
        acc[here, :] += share

    sums = jnp.sum(acc[...].T, axis=0, keepdims=True)
    out_ref[...] = jnp.broadcast_to(sums[None], out_ref.shape)


def in_vmem(count):
    return [pl.BlockSpec(memory_space=pltpu.VMEM)] * count


def in_hbm(count):
    return [pl.BlockSpec(memory_space=pltpu.HBM)] * count


def keep_in(space, array):
    return pltpu.with_memory_space_constraint(array, space)


def gram_cost(nrows, grad):
    blocks, _, _, width = grad.shape
    return pl.CostEstimate(
        flops=nrows * blocks * BLK * 4 * TILE * (TILE + width),
        bytes_accessed=grad.size * 2,
        transcendentals=0,
    )


def gram_early(rows, ids, kinds, pairs, grad):
    every = grad.shape[1]
    tiles = pairs.shape[1] // PARTS
    return pl.pallas_call(
        functools.partial(early_kernel, kinds),
        out_shape=[
            jax.ShapeDtypeStruct((every * DOCS, BLK), jnp.float32),
            pltpu.VMEM(grad.shape, grad.dtype),
        ],
        grid_spec=pltpu.PrefetchScalarGridSpec(
            num_scalar_prefetch=1,
            grid=(),
            in_specs=[*in_vmem(1), *in_hbm(2)],
            out_specs=in_vmem(2),
            scratch_shapes=[
                pltpu.VMEM((AHEAD + 1, tiles, TILE, TILE), jnp.float32),
                pltpu.SemaphoreType.DMA((len(kinds) * PARTS,)),
                pltpu.SemaphoreType.DMA((every * PARTS,)),
            ],
        ),
        compiler_params=pltpu.CompilerParams(vmem_limit_bytes=8 * 2**20),
        cost_estimate=gram_cost(len(kinds), grad),
        name="gram",
    )(rows, ids, keep_in(pltpu.HBM, pairs), keep_in(pltpu.HBM, grad))


def gram_late(rows, ids, first, row, hidden, grad, init, devices):
    return pl.pallas_call(
        functools.partial(late_kernel, row),
        out_shape=jax.ShapeDtypeStruct((devices, 1, BLK), jnp.float32),
        grid_spec=pltpu.PrefetchScalarGridSpec(
            num_scalar_prefetch=1,
            grid=(),
            in_specs=in_vmem(2 + len(hidden) + 2),
            out_specs=pl.BlockSpec(memory_space=pltpu.VMEM),
            scratch_shapes=[pltpu.VMEM(init.shape, jnp.float32)],
        ),
        compiler_params=pltpu.CompilerParams(vmem_limit_bytes=4 * 2**20),
        cost_estimate=gram_cost(1, grad),
        name="gram_late",
    )(rows, ids, first, *hidden, keep_in(pltpu.VMEM, grad), init)


def product_kernel(nrows, bound, rows_ref, ids_ref, norms_ref, *refs):
    pieces = refs[: HALVES * nrows]
    g_ref, out_ref, h_ref, h_sems, factor, scaled = refs[HALVES * nrows :]
    blocks = g_ref.shape[0]
    steps = blocks // DEPTH

    def hidden_copies(k):
        return [
            pltpu.make_async_copy(pieces[n], h_ref.at[n], h_sems.at[n])
            for n in range(HALVES * k, HALVES * (k + 1))
        ]

    for piece in hidden_copies(0):
        piece.start()
    norms = jnp.sum(norms_ref[...], axis=0)
    clip = bound / jnp.maximum(jnp.sqrt(norms), bound) / nrows
    for k in range(nrows):
        ids = ids_ref[:, k, :] + rows_ref[k] * DOCS
        table = jnp.broadcast_to(clip, ids.shape)
        factor[k] = jnp.take_along_axis(table, ids, axis=1)

    def scale(n, slot):
        k, begin = n // steps, n % steps * DEPTH
        lines = jnp.concatenate([factor[k, begin : begin + DEPTH, :]] * (BLK // DEPTH), axis=0).T
        for j in range(DEPTH):
            factors = jnp.broadcast_to(lines[:, j : j + 1], (BLK, BLK))
            for c in range(0, g_ref.shape[3], BLK):
                grad = g_ref[begin + j, k, :, c : c + BLK].astype(jnp.float32)
                scaled[slot, j * BLK : (j + 1) * BLK, c : c + BLK] = (grad * factors).astype(jnp.bfloat16)

    scale(0, 0)
    for n in range(nrows * steps):
        k, begin = n // steps, n % steps * DEPTH
        if begin == 0:
            for piece in hidden_copies(k):
                piece.wait()
            if k + 1 < nrows:
                for piece in hidden_copies(k + 1):
                    piece.start()
        if n + 1 < nrows * steps:
            scale(n + 1, (n + 1) % 2)
        share = lax.dot_general(
            columns_of([h_ref.at[HALVES * k + q] for q in range(HALVES)], begin, DEPTH),
            scaled[n % 2],
            TN,
            preferred_element_type=jnp.float32,
        )
        if n == 0:
            out_ref[...] = share
        else:
            out_ref[...] += share


def product(rows, ids, norms, hidden, grad, bound):
    blocks, nrows, _, width = grad.shape
    pieces = [piece for row in hidden for piece in row]
    return pl.pallas_call(
        functools.partial(product_kernel, nrows, bound),
        out_shape=jax.ShapeDtypeStruct((TILE, width), jnp.float32),
        grid_spec=pltpu.PrefetchScalarGridSpec(
            num_scalar_prefetch=1,
            grid=(),
            in_specs=[*in_vmem(2), *in_hbm(len(pieces)), *in_vmem(1)],
            out_specs=pl.BlockSpec(memory_space=pltpu.VMEM),
            scratch_shapes=[
                pltpu.VMEM((len(pieces), *pieces[0].shape), grad.dtype),
                pltpu.SemaphoreType.DMA((len(pieces),)),
                pltpu.VMEM((nrows, blocks, BLK), jnp.float32),
                pltpu.VMEM((2, DEPTH * BLK, width), jnp.bfloat16),
            ],
        ),
        compiler_params=pltpu.CompilerParams(vmem_limit_bytes=14 * 2**20),
        cost_estimate=pl.CostEstimate(
            flops=2 * nrows * blocks * BLK * TILE * width,
            bytes_accessed=nrows * blocks * BLK * 2 * (TILE + width),
            transcendentals=0,
        ),
        name="product",
    )(rows, ids, norms, *pieces, keep_in(pltpu.VMEM, grad))


def quarters_kernel(me_ref, ids_ref, *refs):
    ins, outs = refs[: len(refs) // 2], refs[len(refs) // 2 :]
    tokens = ins[0].shape[0]
    for in_ref, out_ref in zip(ins, outs):
        out_ref[:tokens, :] = in_ref[...]
        ids = ids_ref[...].astype(jnp.float32).astype(jnp.bfloat16)
        out_ref[tokens:, :BLK] = jnp.broadcast_to(ids, (16, BLK))
        out_ref[tokens:, BLK:] = jnp.zeros((16, out_ref.shape[1] - BLK), jnp.bfloat16)


def quarters(me, offsets, grad, ids):
    tokens, width = grad.shape
    count = len(offsets)
    part = width // count
    return pl.pallas_call(
        quarters_kernel,
        out_shape=[jax.ShapeDtypeStruct((tokens + 16, part), grad.dtype)] * count,
        grid_spec=pltpu.PrefetchScalarGridSpec(
            num_scalar_prefetch=1,
            grid=(1,),
            in_specs=[pl.BlockSpec(ids.shape, lambda i, m: (0, 0))]
            + [
                pl.BlockSpec((tokens, part), lambda i, m, o=o: (0, lax.rem(m[0] + o, count)))
                for o in offsets
            ],
            out_specs=[pl.BlockSpec((tokens + 16, part), lambda i, m: (0, 0))] * count,
        ),
        name="quarters",
    )(me, ids, *[grad] * count)


def columns_kernel(in_ref, *out_refs):
    for j in range(out_refs[0].shape[0]):
        for q, out_ref in enumerate(out_refs):
            at = (j * HALVES + q) * BLK
            out_ref[j] = in_ref[:, at : at + BLK]


def columns(hidden, blocks, steps=4):
    tokens, width = hidden.shape
    count = blocks // steps
    return pl.pallas_call(
        columns_kernel,
        out_shape=[jax.ShapeDtypeStruct((blocks, tokens, BLK), hidden.dtype)] * HALVES,
        grid=(steps,),
        in_specs=[pl.BlockSpec((tokens, width // steps), lambda i: (0, i))],
        out_specs=[pl.BlockSpec((count, tokens, BLK), lambda i: (i, 0, 0))] * HALVES,
        name="columns",
    )(hidden)


def shift(block, distance):
    size = lax.axis_size("dp")
    return lax.ppermute(block, "dp", [(i, (i + distance) % size) for i in range(size)])


def starts(ids):
    docs = jnp.arange(DOCS, dtype=jnp.int32)
    before = jnp.sum((ids[None] < docs[:, None, None, None]).astype(jnp.int32), axis=(1, 3))
    own = ids[None] == docs[:, None, None, None]
    return jnp.sum(jnp.where(own, before[:, None, :, None], 0), axis=0)


def body(hidden, grad_out, segment):
    row_count = lax.axis_size("dp")
    blocks = lax.axis_size("ctx")
    tokens, width_hidden = hidden.shape[1:]
    width_grad = grad_out.shape[2]
    me = lax.axis_index("dp")

    keep, up, down, across = quarters(me[None], (0, 1, 3, 2), grad_out[0], segment)
    across = shift(across, 2)
    received = [keep, shift(up, 1), shift(down, -1), across]

    chunks = columns(hidden[0], blocks)
    chunks, received = lax.optimization_barrier((chunks, received))

    every_grad = jnp.stack([part[:tokens] for part in received])
    every_grad = lax.all_gather(every_grad, "ctx", axis=0, tiled=False)

    hidden_rows = [[], [], [], []]
    ready = None
    for q, chunk in enumerate(chunks):
        if ready is not None:
            chunk, ready = lax.optimization_barrier((chunk, ready))
        own = lax.all_to_all(chunk, "ctx", 0, 0, tiled=True)
        ready = own
        below, above = lax.optimization_barrier((shift(own, 1), shift(own, -1)))
        far = shift(below, 1) if q < HALVES // 2 else shift(above, -1)
        for row, piece in zip(hidden_rows, (own, below, above, far)):
            row.append(piece)

    ids = jnp.stack([part[tokens, :BLK] for part in received]).astype(jnp.int32)
    ids, ready = lax.optimization_barrier((ids, ready))
    ids = jnp.broadcast_to(ids[None], (blocks, row_count, tokens))
    ids = lax.all_to_all(ids, "ctx", 0, 0, tiled=True)
    first = starts(ids)

    rows = lax.rem(me + jnp.array([0, 3, 1, 2], jnp.int32), row_count)
    kinds = (0, 1, 2)
    pairs = hidden_gram(first, kinds, hidden_rows[:3])
    early, grads = gram_early(rows, ids, kinds, pairs, every_grad)
    devices = row_count * blocks
    partial = gram_late(rows, ids, first, 3, hidden_rows[3], grads, early, devices)
    norms = lax.all_to_all(partial, ("dp", "ctx"), 0, 0, tiled=True)

    bound = math.sqrt(tokens * width_hidden * width_grad)
    return product(rows, ids, norms, hidden_rows, grads, bound)


def solution(mesh):
    in_specs = (P("dp", "ctx", None), P("dp", "ctx", None), P("dp", "ctx"))
    out_specs = P("ctx", "dp")
    return jax.shard_map(body, mesh=mesh, in_specs=in_specs, out_specs=out_specs, check_vma=False)
```

```python
import functools
import math

import jax
import jax.numpy as jnp
from jax import lax
from jax.experimental import pallas as pl
from jax.experimental.pallas import tpu as pltpu
from jax.sharding import PartitionSpec as P

BLK = 128
TILE = 256
DOCS = 32
DEPTH = 8
HALVES = 2
PARTS = 4
AHEAD = 6

NT = (((1,), (1,)), ((), ()))
TN = (((0,), (0,)), ((), ()))


def flat(block):
    return block.reshape(block.shape[0] * block.shape[1], block.shape[2])


def columns_of(refs, at, count):
    return jnp.concatenate([flat(ref[pl.ds(at, count)]) for ref in refs], axis=1)


def gram_dot(left, right):
    return lax.dot_general(left, right, NT, preferred_element_type=jnp.float32)


def places():
    spot = lax.broadcasted_iota(jnp.int32, (TILE, TILE), 0)
    column = lax.broadcasted_iota(jnp.int32, (TILE, TILE), 1)
    return spot, column


def pair_products(old, own):
    spot, column = places()
    return jnp.where(spot <= column, gram_dot(own, own), gram_dot(old, own))


def counted(pairs, first):
    spot, column = places()
    weight = jnp.where(spot == column, jnp.float32(1.0), jnp.float32(2.0))
    begin = jnp.where(spot <= column, first, first + TILE)
    return jnp.where(spot >= begin, pairs * weight, jnp.float32(0.0))


def line_of(ref, at, row):
    line = slice(row, row + 1)
    return jnp.concatenate([ref[at, line], ref[at + 1, line]], axis=1)


def doc_sums(terms, ids):
    docs = lax.broadcasted_iota(jnp.int32, (DOCS, TILE), 0)
    total = jnp.sum(terms, axis=0, keepdims=True)
    parts = jnp.where(docs == ids, jnp.broadcast_to(total, docs.shape), jnp.float32(0.0))
    return parts[:, :BLK] + parts[:, BLK:]


def hidden_kernel(kinds, first_ref, *refs):
    per_row = 2 * HALVES
    out_ref = refs[-1]
    tiles = out_ref.shape[1]
    step = pl.program_id(0)
    for k, row in enumerate(kinds):
        row_refs = refs[per_row * k : per_row * (k + 1)]
        old = columns_of(row_refs[HALVES:], 0, 2)
        for t in range(tiles):
            number = step * tiles + t
            first = line_of(first_ref, 2 * number, row) - number * TILE
            own = columns_of(row_refs[:HALVES], 2 * t, 2)
            out_ref[k, t] = counted(pair_products(old, own), first)
            old = own


def hidden_gram(first, kinds, hidden, total, into=None):
    pieces = [piece for row in hidden for piece in row]
    blocks = pieces[0].shape[0]
    count = blocks // PARTS
    tiles = count // 2
    nrows = len(kinds)
    own = pl.BlockSpec((count, BLK, BLK), lambda i: (i, 0, 0))
    old = pl.BlockSpec((2, BLK, BLK), lambda i: (jnp.maximum(i * tiles - 1, 0), 0, 0))
    place = kinds[0] // nrows
    operands = [first, *[piece for row in hidden for piece in [*row, *row]]]
    specs = [
        pl.BlockSpec(first.shape, lambda i: (0, 0, 0)),
        *[spec for _ in kinds for spec in [own] * HALVES + [old] * HALVES],
    ]
    aliases = {}
    if into is not None:
        aliases = {len(operands): 0}
        operands.append(keep_in(pltpu.HBM, into))
        specs.append(pl.BlockSpec(memory_space=pltpu.HBM))
    return pl.pallas_call(
        functools.partial(hidden_kernel, kinds),
        out_shape=pltpu.HBM((total, blocks // 2, TILE, TILE), jnp.float32),
        grid=(PARTS,),
        in_specs=specs,
        out_specs=pl.BlockSpec((nrows, tiles, TILE, TILE), lambda i: (place, i, 0, 0)),
        input_output_aliases=aliases,
        compiler_params=pltpu.CompilerParams(vmem_limit_bytes=24 * 2**20),
        cost_estimate=pl.CostEstimate(
            flops=nrows * blocks * BLK * 4 * TILE * TILE,
            bytes_accessed=nrows * blocks * BLK * TILE * 6,
            transcendentals=0,
        ),
        name="hidden_gram",
    )(*operands)


def early_kernel(kinds, rows_ref, ids_ref, pairs_hbm, g_hbm, out_ref, g_ref, last_ref, pairs_ref, pair_sems, sems):
    nrows = len(kinds)
    blocks, every = g_ref.shape[:2]
    count = blocks // PARTS
    tiles = count // 2

    def copy(n):
        here = pl.ds(lax.rem(n, PARTS) * count, count)
        row = n // PARTS
        return pltpu.make_async_copy(g_hbm.at[here, row], g_ref.at[here, row], sems.at[n])

    def pair_copy(n):
        here = pl.ds(lax.rem(n, PARTS) * tiles, tiles)
        slot = lax.rem(n, AHEAD + 2)
        return pltpu.make_async_copy(pairs_hbm.at[n // PARTS, here], pairs_ref.at[slot], pair_sems.at[n])

    for n in range(AHEAD):
        copy(n).start()
        pair_copy(n).start()
    out_ref[...] = jnp.zeros_like(out_ref)
    for k, row in enumerate(kinds):

        @pl.loop(0, PARTS // 2)
        def _(i, k=k, row=row):
            for n in (k * PARTS + 2 * i, k * PARTS + 2 * i + 1):
                copy(n).wait()
                pair_copy(n).wait()

                @pl.when(n + AHEAD < every * PARTS)
                def _():
                    copy(n + AHEAD).start()

                @pl.when(n + AHEAD < nrows * PARTS)
                def _():
                    pair_copy(n + AHEAD).start()

            share = jnp.zeros((DOCS, BLK), jnp.float32)
            begin = 2 * i * count
            old = flat(g_ref[pl.ds(jnp.maximum(begin - 2, 0), 2), row])
            for t in range(2 * tiles):
                at = begin + 2 * t
                slot = lax.rem(k * PARTS + 2 * i + t // tiles, AHEAD + 2)
                own = flat(g_ref[pl.ds(at, 2), row])
                terms = pairs_ref[slot, t % tiles] * pair_products(old, own)
                share += doc_sums(terms, line_of(ids_ref, at, row))
                old = own
            here = pl.ds(pl.multiple_of(rows_ref[row] * DOCS, DOCS), DOCS)
            out_ref[here, :] += share

    @pl.loop(0, PARTS // 2)
    def _(i):
        for n in (nrows * PARTS + 2 * i, nrows * PARTS + 2 * i + 1):
            copy(n).wait()
        begin = 2 * i * count
        old = flat(g_ref[pl.ds(jnp.maximum(begin - 2, 0), 2), nrows])
        for t in range(2 * tiles):
            own = flat(g_ref[pl.ds(begin + 2 * t, 2), nrows])
            last_ref[2 * i * tiles + t] = pair_products(old, own)
            old = own


def late_kernel(row, rows_ref, ids_ref, first_ref, *refs):
    h_refs = refs[:HALVES]
    last_ref, init_ref, out_ref, acc = refs[HALVES:]
    tiles = last_ref.shape[0] // 2
    acc[...] = init_ref[...]

    @pl.loop(0, 2)
    def _(i):
        share = jnp.zeros((DOCS, BLK), jnp.float32)
        old = columns_of(h_refs, jnp.maximum(2 * i * tiles - 2, 0), 2)
        for t in range(tiles):
            number = i * tiles + t
            first = line_of(first_ref, 2 * number, row) - number * TILE
            own = columns_of(h_refs, 2 * number, 2)
            terms = counted(pair_products(old, own), first) * last_ref[number]
            share += doc_sums(terms, line_of(ids_ref, 2 * number, row))
            old = own
        here = pl.ds(pl.multiple_of(rows_ref[row] * DOCS, DOCS), DOCS)
        acc[here, :] += share

    sums = jnp.sum(acc[...].T, axis=0, keepdims=True)
    out_ref[...] = jnp.broadcast_to(sums[None], out_ref.shape)


def in_vmem(count):
    return [pl.BlockSpec(memory_space=pltpu.VMEM)] * count


def in_hbm(count):
    return [pl.BlockSpec(memory_space=pltpu.HBM)] * count


def keep_in(space, array):
    return pltpu.with_memory_space_constraint(array, space)


def gram_cost(nrows, grad):
    blocks, _, _, width = grad.shape
    return pl.CostEstimate(
        flops=nrows * blocks * BLK * 4 * TILE * (TILE + width),
        bytes_accessed=grad.size * 2,
        transcendentals=0,
    )


def gram_early(rows, ids, kinds, pairs, grad):
    every = grad.shape[1]
    tiles = pairs.shape[1] // PARTS
    return pl.pallas_call(
        functools.partial(early_kernel, kinds),
        out_shape=[
            jax.ShapeDtypeStruct((every * DOCS, BLK), jnp.float32),
            pltpu.VMEM(grad.shape, grad.dtype),
            pltpu.VMEM((pairs.shape[1], TILE, TILE), jnp.float32),
        ],
        grid_spec=pltpu.PrefetchScalarGridSpec(
            num_scalar_prefetch=1,
            grid=(),
            in_specs=[*in_vmem(1), *in_hbm(2)],
            out_specs=in_vmem(3),
            scratch_shapes=[
                pltpu.VMEM((AHEAD + 2, tiles, TILE, TILE), jnp.float32),
                pltpu.SemaphoreType.DMA((len(kinds) * PARTS,)),
                pltpu.SemaphoreType.DMA((every * PARTS,)),
            ],
        ),
        compiler_params=pltpu.CompilerParams(vmem_limit_bytes=12 * 2**20),
        cost_estimate=gram_cost(len(kinds), grad),
        name="gram",
    )(rows, ids, keep_in(pltpu.HBM, pairs), keep_in(pltpu.HBM, grad))


def gram_late(rows, ids, first, row, hidden, last, init, devices):
    return pl.pallas_call(
        functools.partial(late_kernel, row),
        out_shape=jax.ShapeDtypeStruct((devices, 1, BLK), jnp.float32),
        grid_spec=pltpu.PrefetchScalarGridSpec(
            num_scalar_prefetch=1,
            grid=(),
            in_specs=in_vmem(2 + len(hidden) + 2),
            out_specs=pl.BlockSpec(memory_space=pltpu.VMEM),
            scratch_shapes=[pltpu.VMEM(init.shape, jnp.float32)],
        ),
        compiler_params=pltpu.CompilerParams(vmem_limit_bytes=8 * 2**20),
        cost_estimate=pl.CostEstimate(
            flops=2 * 2 * last.size * TILE, bytes_accessed=last.size * 4, transcendentals=0
        ),
        name="gram_late",
    )(rows, ids, first, *hidden, keep_in(pltpu.VMEM, last), init)


def product_kernel(nrows, bound, rows_ref, ids_ref, norms_ref, *refs):
    pieces = refs[: HALVES * nrows]
    g_ref, out_ref, h_ref, h_sems, factor, scaled = refs[HALVES * nrows :]
    blocks = g_ref.shape[0]
    steps = blocks // DEPTH

    order = [nrows - 2, *range(nrows - 2), nrows - 1]

    def hidden_copies(k):
        return [
            pltpu.make_async_copy(pieces[n], h_ref.at[n], h_sems.at[n])
            for n in range(HALVES * k, HALVES * (k + 1))
        ]

    for piece in hidden_copies(order[0]):
        piece.start()
    norms = jnp.sum(norms_ref[...], axis=0)
    clip = bound / jnp.maximum(jnp.sqrt(norms), bound) / nrows
    for k in range(nrows):
        ids = ids_ref[:, k, :] + rows_ref[k] * DOCS
        table = jnp.broadcast_to(clip, ids.shape)
        factor[k] = jnp.take_along_axis(table, ids, axis=1)

    def scale(n, slot):
        k, begin = order[n // steps], n % steps * DEPTH
        lines = jnp.concatenate([factor[k, begin : begin + DEPTH, :]] * (BLK // DEPTH), axis=0).T
        for j in range(DEPTH):
            factors = jnp.broadcast_to(lines[:, j : j + 1], (BLK, BLK))
            for c in range(0, g_ref.shape[3], BLK):
                grad = g_ref[begin + j, k, :, c : c + BLK].astype(jnp.float32)
                scaled[slot, j * BLK : (j + 1) * BLK, c : c + BLK] = (grad * factors).astype(jnp.bfloat16)

    scale(0, 0)
    for n in range(nrows * steps):
        k, begin = order[n // steps], n % steps * DEPTH
        if begin == 0:
            for piece in hidden_copies(k):
                piece.wait()
            if n // steps + 1 < nrows:
                for piece in hidden_copies(order[n // steps + 1]):
                    piece.start()
        if n + 1 < nrows * steps:
            scale(n + 1, (n + 1) % 2)
        share = lax.dot_general(
            columns_of([h_ref.at[HALVES * k + q] for q in range(HALVES)], begin, DEPTH),
            scaled[n % 2],
            TN,
            preferred_element_type=jnp.float32,
        )
        if n == 0:
            out_ref[...] = share
        else:
            out_ref[...] += share


def product(rows, ids, norms, hidden, grad, bound):
    blocks, nrows, _, width = grad.shape
    pieces = [piece for row in hidden for piece in row]
    return pl.pallas_call(
        functools.partial(product_kernel, nrows, bound),
        out_shape=jax.ShapeDtypeStruct((TILE, width), jnp.float32),
        grid_spec=pltpu.PrefetchScalarGridSpec(
            num_scalar_prefetch=1,
            grid=(),
            in_specs=[*in_vmem(2), *in_hbm(len(pieces)), *in_vmem(1)],
            out_specs=pl.BlockSpec(memory_space=pltpu.VMEM),
            scratch_shapes=[
                pltpu.VMEM((len(pieces), *pieces[0].shape), grad.dtype),
                pltpu.SemaphoreType.DMA((len(pieces),)),
                pltpu.VMEM((nrows, blocks, BLK), jnp.float32),
                pltpu.VMEM((2, DEPTH * BLK, width), jnp.bfloat16),
            ],
        ),
        compiler_params=pltpu.CompilerParams(vmem_limit_bytes=14 * 2**20),
        cost_estimate=pl.CostEstimate(
            flops=2 * nrows * blocks * BLK * TILE * width,
            bytes_accessed=nrows * blocks * BLK * 2 * (TILE + width),
            transcendentals=0,
        ),
        name="product",
    )(rows, ids, norms, *pieces, keep_in(pltpu.VMEM, grad))


def quarters_kernel(me_ref, ids_ref, *refs):
    ins, outs = refs[: len(refs) // 2], refs[len(refs) // 2 :]
    tokens = ins[0].shape[0]
    for in_ref, out_ref in zip(ins, outs):
        out_ref[:tokens, :] = in_ref[...]
        ids = ids_ref[...].astype(jnp.float32).astype(jnp.bfloat16)
        out_ref[tokens:, :BLK] = jnp.broadcast_to(ids, (16, BLK))
        out_ref[tokens:, BLK:] = jnp.zeros((16, out_ref.shape[1] - BLK), jnp.bfloat16)


def quarters(me, offsets, grad, ids):
    tokens, width = grad.shape
    count = len(offsets)
    part = width // count
    return pl.pallas_call(
        quarters_kernel,
        out_shape=[jax.ShapeDtypeStruct((tokens + 16, part), grad.dtype)] * count,
        grid_spec=pltpu.PrefetchScalarGridSpec(
            num_scalar_prefetch=1,
            grid=(1,),
            in_specs=[pl.BlockSpec(ids.shape, lambda i, m: (0, 0))]
            + [
                pl.BlockSpec((tokens, part), lambda i, m, o=o: (0, lax.rem(m[0] + o, count)))
                for o in offsets
            ],
            out_specs=[pl.BlockSpec((tokens + 16, part), lambda i, m: (0, 0))] * count,
        ),
        name="quarters",
    )(me, ids, *[grad] * count)


def columns_kernel(in_ref, *out_refs):
    for j in range(out_refs[0].shape[0]):
        for q, out_ref in enumerate(out_refs):
            at = (j * HALVES + q) * BLK
            out_ref[j] = in_ref[:, at : at + BLK]


def columns(hidden, blocks, steps=4):
    tokens, width = hidden.shape
    count = blocks // steps
    return pl.pallas_call(
        columns_kernel,
        out_shape=[jax.ShapeDtypeStruct((blocks, tokens, BLK), hidden.dtype)] * HALVES,
        grid=(steps,),
        in_specs=[pl.BlockSpec((tokens, width // steps), lambda i: (0, i))],
        out_specs=[pl.BlockSpec((count, tokens, BLK), lambda i: (i, 0, 0))] * HALVES,
        name="columns",
    )(hidden)


def shift(block, distance):
    size = lax.axis_size("dp")
    return lax.ppermute(block, "dp", [(i, (i + distance) % size) for i in range(size)])


def starts(ids):
    docs = jnp.arange(DOCS, dtype=jnp.int32)
    before = jnp.sum((ids[None] < docs[:, None, None, None]).astype(jnp.int32), axis=(1, 3))
    own = ids[None] == docs[:, None, None, None]
    return jnp.sum(jnp.where(own, before[:, None, :, None], 0), axis=0)


def body(hidden, grad_out, segment):
    row_count = lax.axis_size("dp")
    blocks = lax.axis_size("ctx")
    tokens, width_hidden = hidden.shape[1:]
    width_grad = grad_out.shape[2]
    me = lax.axis_index("dp")

    keep, up, down, across = quarters(me[None], (0, 1, 3, 2), grad_out[0], segment)
    across = shift(across, 2)
    received = [shift(up, 1), shift(down, -1), keep, across]

    chunks = columns(hidden[0], blocks)
    received, _ = lax.optimization_barrier((received, chunks))

    every_grad = jnp.stack([part[:tokens] for part in received])
    every_grad = lax.all_gather(every_grad, "ctx", axis=0, tiled=False)

    hidden_rows = [[], [], [], []]
    ready = None
    for q, chunk in enumerate(chunks):
        if ready is not None:
            chunk, ready = lax.optimization_barrier((chunk, ready))
        own = lax.all_to_all(chunk, "ctx", 0, 0, tiled=True)
        ready = own
        below, above = lax.optimization_barrier((shift(own, 1), shift(own, -1)))
        far = shift(below, 1) if q < HALVES // 2 else shift(above, -1)
        for row, piece in zip(hidden_rows, (below, above, own, far)):
            row.append(piece)

    ids = jnp.stack([part[tokens, :BLK] for part in received]).astype(jnp.int32)
    ids, ready = lax.optimization_barrier((ids, ready))
    ids = jnp.broadcast_to(ids[None], (blocks, row_count, tokens))
    ids = lax.all_to_all(ids, "ctx", 0, 0, tiled=True)
    first = starts(ids)

    rows = lax.rem(me + jnp.array([3, 1, 0, 2], jnp.int32), row_count)
    kinds = (0, 1, 2)
    pairs = hidden_gram(first, kinds[2:], hidden_rows[2:3], len(kinds))
    pairs = hidden_gram(first, kinds[:2], hidden_rows[:2], len(kinds), pairs)
    early, grads, last = gram_early(rows, ids, kinds, pairs, every_grad)
    devices = row_count * blocks
    partial = gram_late(rows, ids, first, 3, hidden_rows[3], last, early, devices)
    norms = lax.all_to_all(partial, ("dp", "ctx"), 0, 0, tiled=True)

    bound = math.sqrt(tokens * width_hidden * width_grad)
    return product(rows, ids, norms, hidden_rows, grads, bound)


def solution(mesh):
    in_specs = (P("dp", "ctx", None), P("dp", "ctx", None), P("dp", "ctx"))
    out_specs = P("ctx", "dp")
    return jax.shard_map(body, mesh=mesh, in_specs=in_specs, out_specs=out_specs, check_vma=False)
```

```python
import functools
import math

import jax
import jax.numpy as jnp
from jax import lax
from jax.experimental import pallas as pl
from jax.experimental.pallas import tpu as pltpu
from jax.sharding import PartitionSpec as P

BLK = 128
TILE = 256
DOCS = 32
DEPTH = 8
HALVES = 2
PARTS = 4
AHEAD = 6

NT = (((1,), (1,)), ((), ()))
TN = (((0,), (0,)), ((), ()))


def flat(block):
    return block.reshape(block.shape[0] * block.shape[1], block.shape[2])


def columns_of(refs, at, count):
    return jnp.concatenate([flat(ref[pl.ds(at, count)]) for ref in refs], axis=1)


def gram_dot(left, right):
    return lax.dot_general(left, right, NT, preferred_element_type=jnp.float32)


def places():
    spot = lax.broadcasted_iota(jnp.int32, (TILE, TILE), 0)
    column = lax.broadcasted_iota(jnp.int32, (TILE, TILE), 1)
    return spot, column


def pair_products(old, own):
    spot, column = places()
    return jnp.where(spot <= column, gram_dot(own, own), gram_dot(old, own))


def counted(pairs, first):
    spot, column = places()
    weight = jnp.where(spot == column, jnp.float32(1.0), jnp.float32(2.0))
    begin = jnp.where(spot <= column, first, first + TILE)
    return jnp.where(spot >= begin, pairs * weight, jnp.float32(0.0))


def line_of(ref, at, row):
    line = slice(row, row + 1)
    return jnp.concatenate([ref[at, line], ref[at + 1, line]], axis=1)


def doc_sums(terms, ids):
    docs = lax.broadcasted_iota(jnp.int32, (DOCS, TILE), 0)
    total = jnp.sum(terms, axis=0, keepdims=True)
    parts = jnp.where(docs == ids, jnp.broadcast_to(total, docs.shape), jnp.float32(0.0))
    return parts[:, :BLK] + parts[:, BLK:]


def hidden_kernel(kinds, first_ref, *refs):
    per_row = 2 * HALVES
    out_ref = refs[-1]
    tiles = out_ref.shape[1]
    step = pl.program_id(0)
    for k, row in enumerate(kinds):
        row_refs = refs[per_row * k : per_row * (k + 1)]
        old = columns_of(row_refs[HALVES:], 0, 2)
        for t in range(tiles):
            number = step * tiles + t
            first = line_of(first_ref, 2 * number, row) - number * TILE
            own = columns_of(row_refs[:HALVES], 2 * t, 2)
            out_ref[k, t] = counted(pair_products(old, own), first)
            old = own


def hidden_gram(first, kinds, hidden, total, into=None):
    pieces = [piece for row in hidden for piece in row]
    blocks = pieces[0].shape[0]
    count = blocks // PARTS
    tiles = count // 2
    nrows = len(kinds)
    own = pl.BlockSpec((count, BLK, BLK), lambda i: (i, 0, 0))
    old = pl.BlockSpec((2, BLK, BLK), lambda i: (jnp.maximum(i * tiles - 1, 0), 0, 0))
    place = kinds[0] // nrows
    operands = [first, *[piece for row in hidden for piece in [*row, *row]]]
    specs = [
        pl.BlockSpec(first.shape, lambda i: (0, 0, 0)),
        *[spec for _ in kinds for spec in [own] * HALVES + [old] * HALVES],
    ]
    aliases = {}
    if into is not None:
        aliases = {len(operands): 0}
        operands.append(keep_in(pltpu.HBM, into))
        specs.append(pl.BlockSpec(memory_space=pltpu.HBM))
    return pl.pallas_call(
        functools.partial(hidden_kernel, kinds),
        out_shape=pltpu.HBM((total, blocks // 2, TILE, TILE), jnp.float32),
        grid=(PARTS,),
        in_specs=specs,
        out_specs=pl.BlockSpec((nrows, tiles, TILE, TILE), lambda i: (place, i, 0, 0)),
        input_output_aliases=aliases,
        compiler_params=pltpu.CompilerParams(vmem_limit_bytes=24 * 2**20),
        cost_estimate=pl.CostEstimate(
            flops=nrows * blocks * BLK * 4 * TILE * TILE,
            bytes_accessed=nrows * blocks * BLK * TILE * 6,
            transcendentals=0,
        ),
        name="hidden_gram",
    )(*operands)


def early_kernel(kinds, rows_ref, ids_ref, pairs_hbm, g_hbm, out_ref, g_ref, last_ref, pairs_ref, pair_sems, sems):
    nrows = len(kinds)
    blocks, every = g_ref.shape[:2]
    count = blocks // PARTS
    tiles = count // 2

    def copy(n):
        here = pl.ds(lax.rem(n, PARTS) * count, count)
        row = n // PARTS
        return pltpu.make_async_copy(g_hbm.at[here, row], g_ref.at[here, row], sems.at[n])

    def pair_copy(n):
        here = pl.ds(lax.rem(n, PARTS) * tiles, tiles)
        slot = lax.rem(n, AHEAD + 2)
        return pltpu.make_async_copy(pairs_hbm.at[n // PARTS, here], pairs_ref.at[slot], pair_sems.at[n])

    for n in range(AHEAD):
        copy(n).start()
        pair_copy(n).start()
    out_ref[...] = jnp.zeros_like(out_ref)

    def add(k, row, c, parts):
        for n in (k * PARTS + c + p for p in range(parts)):
            copy(n).wait()
            pair_copy(n).wait()

            @pl.when(n + AHEAD < every * PARTS)
            def _():
                copy(n + AHEAD).start()

            @pl.when(n + AHEAD < nrows * PARTS)
            def _():
                pair_copy(n + AHEAD).start()

        share = jnp.zeros((DOCS, BLK), jnp.float32)
        begin = c * count
        old = flat(g_ref[pl.ds(jnp.maximum(begin - 2, 0), 2), row])
        for t in range(parts * tiles):
            at = begin + 2 * t
            slot = lax.rem(k * PARTS + c + t // tiles, AHEAD + 2)
            own = flat(g_ref[pl.ds(at, 2), row])
            terms = pairs_ref[slot, t % tiles] * pair_products(old, own)
            share += doc_sums(terms, line_of(ids_ref, at, row))
            old = own
        here = pl.ds(pl.multiple_of(rows_ref[row] * DOCS, DOCS), DOCS)
        out_ref[here, :] += share

    for k, row in enumerate(kinds):
        if k == 0:
            pl.loop(0, 2)(lambda c, k=k, row=row: add(k, row, c, 1))
            add(k, row, 2, PARTS - 2)
        else:
            pl.loop(0, PARTS // 2)(lambda i, k=k, row=row: add(k, row, 2 * i, 2))

    @pl.loop(0, PARTS // 2)
    def _(i):
        for n in (nrows * PARTS + 2 * i, nrows * PARTS + 2 * i + 1):
            copy(n).wait()
        begin = 2 * i * count
        old = flat(g_ref[pl.ds(jnp.maximum(begin - 2, 0), 2), nrows])
        for t in range(2 * tiles):
            own = flat(g_ref[pl.ds(begin + 2 * t, 2), nrows])
            last_ref[2 * i * tiles + t] = pair_products(old, own)
            old = own


def late_kernel(row, rows_ref, ids_ref, first_ref, *refs):
    pieces = refs[:HALVES]
    last_ref, init_ref, out_ref, acc, h_ref, sems = refs[HALVES:]
    count = h_ref.shape[1] // PARTS
    tiles = count // 2

    def copies(c):
        here = pl.ds(c * count, count)
        return [
            pltpu.make_async_copy(piece.at[here], h_ref.at[q, here], sems.at[c, q])
            for q, piece in enumerate(pieces)
        ]

    for c in range(PARTS):
        for copy in copies(c):
            copy.start()
    acc[...] = init_ref[...]
    h_refs = [h_ref.at[q] for q in range(HALVES)]
    share = jnp.zeros((DOCS, BLK), jnp.float32)
    for c in range(PARTS):
        for copy in copies(c):
            copy.wait()
        old = columns_of(h_refs, max(c * count - 2, 0), 2)
        for t in range(tiles):
            number = c * tiles + t
            first = line_of(first_ref, 2 * number, row) - number * TILE
            own = columns_of(h_refs, 2 * number, 2)
            terms = counted(pair_products(old, own), first) * last_ref[number]
            share += doc_sums(terms, line_of(ids_ref, 2 * number, row))
            old = own
    here = pl.ds(pl.multiple_of(rows_ref[row] * DOCS, DOCS), DOCS)
    acc[here, :] += share

    sums = jnp.sum(acc[...].T, axis=0, keepdims=True)
    out_ref[...] = jnp.broadcast_to(sums[None], out_ref.shape)


def in_vmem(count):
    return [pl.BlockSpec(memory_space=pltpu.VMEM)] * count


def in_hbm(count):
    return [pl.BlockSpec(memory_space=pltpu.HBM)] * count


def keep_in(space, array):
    return pltpu.with_memory_space_constraint(array, space)


def gram_cost(nrows, grad):
    blocks, _, _, width = grad.shape
    return pl.CostEstimate(
        flops=nrows * blocks * BLK * 4 * TILE * (TILE + width),
        bytes_accessed=grad.size * 2,
        transcendentals=0,
    )


def gram_early(rows, ids, kinds, pairs, grad):
    every = grad.shape[1]
    tiles = pairs.shape[1] // PARTS
    return pl.pallas_call(
        functools.partial(early_kernel, kinds),
        out_shape=[
            jax.ShapeDtypeStruct((every * DOCS, BLK), jnp.float32),
            pltpu.VMEM(grad.shape, grad.dtype),
            pltpu.VMEM((pairs.shape[1], TILE, TILE), jnp.float32),
        ],
        grid_spec=pltpu.PrefetchScalarGridSpec(
            num_scalar_prefetch=1,
            grid=(),
            in_specs=[*in_vmem(1), *in_hbm(2)],
            out_specs=in_vmem(3),
            scratch_shapes=[
                pltpu.VMEM((AHEAD + 2, tiles, TILE, TILE), jnp.float32),
                pltpu.SemaphoreType.DMA((len(kinds) * PARTS,)),
                pltpu.SemaphoreType.DMA((every * PARTS,)),
            ],
        ),
        compiler_params=pltpu.CompilerParams(vmem_limit_bytes=12 * 2**20),
        cost_estimate=gram_cost(len(kinds), grad),
        name="gram",
    )(rows, ids, keep_in(pltpu.HBM, pairs), keep_in(pltpu.HBM, grad))


def gram_late(rows, ids, first, row, hidden, last, init, devices):
    return pl.pallas_call(
        functools.partial(late_kernel, row),
        out_shape=jax.ShapeDtypeStruct((devices, 1, BLK), jnp.float32),
        grid_spec=pltpu.PrefetchScalarGridSpec(
            num_scalar_prefetch=1,
            grid=(),
            in_specs=[*in_vmem(2), *in_hbm(len(hidden)), *in_vmem(2)],
            out_specs=pl.BlockSpec(memory_space=pltpu.VMEM),
            scratch_shapes=[
                pltpu.VMEM(init.shape, jnp.float32),
                pltpu.VMEM((len(hidden), *hidden[0].shape), hidden[0].dtype),
                pltpu.SemaphoreType.DMA((PARTS, len(hidden))),
            ],
        ),
        compiler_params=pltpu.CompilerParams(vmem_limit_bytes=8 * 2**20),
        cost_estimate=pl.CostEstimate(
            flops=2 * 2 * last.size * TILE, bytes_accessed=last.size * 4, transcendentals=0
        ),
        name="gram_late",
    )(rows, ids, first, *hidden, keep_in(pltpu.VMEM, last), init)


def product_kernel(nrows, bound, rows_ref, ids_ref, norms_ref, *refs):
    pieces = refs[: HALVES * nrows]
    g_ref, out_ref, h_ref, h_sems, factor, scaled = refs[HALVES * nrows :]
    blocks = g_ref.shape[0]
    steps = blocks // DEPTH

    order = [nrows - 2, *range(nrows - 2), nrows - 1]

    def hidden_copies(k):
        return [
            pltpu.make_async_copy(pieces[n], h_ref.at[n], h_sems.at[n])
            for n in range(HALVES * k, HALVES * (k + 1))
        ]

    for piece in hidden_copies(order[0]):
        piece.start()
    norms = jnp.maximum(jnp.sum(norms_ref[...], axis=0), 0.0)
    clip = bound / jnp.maximum(jnp.sqrt(norms), bound) / nrows
    for k in range(nrows):
        ids = ids_ref[:, k, :] + rows_ref[k] * DOCS
        table = jnp.broadcast_to(clip, ids.shape)
        factor[k] = jnp.take_along_axis(table, ids, axis=1)

    def scale(n, slot):
        k, begin = order[n // steps], n % steps * DEPTH
        lines = jnp.concatenate([factor[k, begin : begin + DEPTH, :]] * (BLK // DEPTH), axis=0).T
        for j in range(DEPTH):
            factors = jnp.broadcast_to(lines[:, j : j + 1], (BLK, BLK))
            for c in range(0, g_ref.shape[3], BLK):
                grad = g_ref[begin + j, k, :, c : c + BLK].astype(jnp.float32)
                scaled[slot, j * BLK : (j + 1) * BLK, c : c + BLK] = (grad * factors).astype(jnp.bfloat16)

    scale(0, 0)
    for n in range(nrows * steps):
        k, begin = order[n // steps], n % steps * DEPTH
        if begin == 0:
            for piece in hidden_copies(k):
                piece.wait()
            if n // steps + 1 < nrows:
                for piece in hidden_copies(order[n // steps + 1]):
                    piece.start()
        if n + 1 < nrows * steps:
            scale(n + 1, (n + 1) % 2)
        share = lax.dot_general(
            columns_of([h_ref.at[HALVES * k + q] for q in range(HALVES)], begin, DEPTH),
            scaled[n % 2],
            TN,
            preferred_element_type=jnp.float32,
        )
        if n == 0:
            out_ref[...] = share
        else:
            out_ref[...] += share


def product(rows, ids, norms, hidden, grad, bound):
    blocks, nrows, _, width = grad.shape
    pieces = [piece for row in hidden for piece in row]
    return pl.pallas_call(
        functools.partial(product_kernel, nrows, bound),
        out_shape=jax.ShapeDtypeStruct((TILE, width), jnp.float32),
        grid_spec=pltpu.PrefetchScalarGridSpec(
            num_scalar_prefetch=1,
            grid=(),
            in_specs=[*in_vmem(2), *in_hbm(len(pieces)), *in_vmem(1)],
            out_specs=pl.BlockSpec(memory_space=pltpu.VMEM),
            scratch_shapes=[
                pltpu.VMEM((len(pieces), *pieces[0].shape), grad.dtype),
                pltpu.SemaphoreType.DMA((len(pieces),)),
                pltpu.VMEM((nrows, blocks, BLK), jnp.float32),
                pltpu.VMEM((2, DEPTH * BLK, width), jnp.bfloat16),
            ],
        ),
        compiler_params=pltpu.CompilerParams(vmem_limit_bytes=14 * 2**20),
        cost_estimate=pl.CostEstimate(
            flops=2 * nrows * blocks * BLK * TILE * width,
            bytes_accessed=nrows * blocks * BLK * 2 * (TILE + width),
            transcendentals=0,
        ),
        name="product",
    )(rows, ids, norms, *pieces, keep_in(pltpu.VMEM, grad))


def quarters_kernel(offsets, me_ref, ids_ref, grad_ref, *refs):
    out_refs, sems = refs[:-1], refs[-1]
    tokens = grad_ref.shape[0]
    part = out_refs[0].shape[1]
    count = len(offsets)
    copies = []
    for n, (offset, out_ref) in enumerate(zip(offsets, out_refs)):
        begin = pl.multiple_of(lax.rem(me_ref[0] + offset, count) * part, BLK)
        source = grad_ref.at[:, pl.ds(begin, part)]
        copies.append(pltpu.make_async_copy(source, out_ref.at[pl.ds(0, tokens)], sems.at[n]))
    for copy in copies:
        copy.start()
    ids = jnp.broadcast_to(ids_ref[...].astype(jnp.float32).astype(jnp.bfloat16), (16, BLK))
    for out_ref in out_refs:
        out_ref[tokens:, :BLK] = ids
        out_ref[tokens:, BLK:] = jnp.zeros((16, part - BLK), jnp.bfloat16)
    for copy in copies:
        copy.wait()


def quarters(me, offsets, grad, ids):
    tokens, width = grad.shape
    count = len(offsets)
    return pl.pallas_call(
        functools.partial(quarters_kernel, offsets),
        out_shape=[pltpu.VMEM((tokens + 16, width // count), grad.dtype)] * count,
        grid_spec=pltpu.PrefetchScalarGridSpec(
            num_scalar_prefetch=1,
            grid=(),
            in_specs=[*in_vmem(1), *in_hbm(1)],
            out_specs=in_vmem(count),
            scratch_shapes=[pltpu.SemaphoreType.DMA((count,))],
        ),
        name="quarters",
    )(me, ids, keep_in(pltpu.HBM, grad))


def columns_kernel(in_ref, *out_refs):
    for j in range(out_refs[0].shape[0]):
        for q, out_ref in enumerate(out_refs):
            at = (j * HALVES + q) * BLK
            out_ref[j] = in_ref[:, at : at + BLK]


def columns(hidden, blocks, steps=4):
    tokens, width = hidden.shape
    count = blocks // steps
    return pl.pallas_call(
        columns_kernel,
        out_shape=[jax.ShapeDtypeStruct((blocks, tokens, BLK), hidden.dtype)] * HALVES,
        grid=(steps,),
        in_specs=[pl.BlockSpec((tokens, width // steps), lambda i: (0, i))],
        out_specs=[pl.BlockSpec((count, tokens, BLK), lambda i: (i, 0, 0))] * HALVES,
        name="columns",
    )(hidden)


def shift(block, distance):
    size = lax.axis_size("dp")
    return lax.ppermute(block, "dp", [(i, (i + distance) % size) for i in range(size)])


def starts(ids):
    docs = jnp.arange(DOCS, dtype=jnp.int32)
    before = jnp.sum((ids[None] < docs[:, None, None, None]).astype(jnp.int32), axis=(1, 3))
    own = ids[None] == docs[:, None, None, None]
    return jnp.sum(jnp.where(own, before[:, None, :, None], 0), axis=0)


def body(hidden, grad_out, segment):
    row_count = lax.axis_size("dp")
    blocks = lax.axis_size("ctx")
    tokens, width_hidden = hidden.shape[1:]
    width_grad = grad_out.shape[2]
    me = lax.axis_index("dp")

    keep, up, down, across = quarters(me[None], (0, 1, 3, 2), grad_out[0], segment)
    received = [shift(up, 1), shift(down, -1), keep, shift(across, 2)]

    chunks = columns(hidden[0], blocks)
    received, _ = lax.optimization_barrier((received, chunks))

    every_grad = jnp.stack([part[:tokens] for part in received])
    every_grad = lax.all_gather(every_grad, "ctx", axis=0, tiled=False)

    hidden_rows = [[], [], [], []]
    ready = None
    for q, chunk in enumerate(chunks):
        if ready is not None:
            chunk, ready = lax.optimization_barrier((chunk, ready))
        own = lax.all_to_all(chunk, "ctx", 0, 0, tiled=True)
        ready = own
        below, above = lax.optimization_barrier((shift(own, 1), shift(own, -1)))
        far = shift(below, 1) if q < HALVES // 2 else shift(above, -1)
        for row, piece in zip(hidden_rows, (below, above, own, far)):
            row.append(piece)

    ids = jnp.stack([part[tokens, :BLK] for part in received]).astype(jnp.int32)
    ids, ready = lax.optimization_barrier((ids, ready))
    ids = jnp.broadcast_to(ids[None], (blocks, row_count, tokens))
    ids = lax.all_to_all(ids, "ctx", 0, 0, tiled=True)
    first = starts(ids)

    rows = lax.rem(me + jnp.array([3, 1, 0, 2], jnp.int32), row_count)
    kinds = (0, 1, 2)
    pairs = hidden_gram(first, kinds[2:], hidden_rows[2:3], len(kinds))
    pairs = hidden_gram(first, kinds[:2], hidden_rows[:2], len(kinds), pairs)
    early, grads, last = gram_early(rows, ids, kinds, pairs, every_grad)
    devices = row_count * blocks
    partial = gram_late(rows, ids, first, 3, hidden_rows[3], last, early, devices)
    norms = lax.all_to_all(partial, ("dp", "ctx"), 0, 0, tiled=True)

    bound = math.sqrt(tokens * width_hidden * width_grad)
    return product(rows, ids, norms, hidden_rows, grads, bound)


def solution(mesh):
    in_specs = (P("dp", "ctx", None), P("dp", "ctx", None), P("dp", "ctx"))
    out_specs = P("ctx", "dp")
    return jax.shard_map(body, mesh=mesh, in_specs=in_specs, out_specs=out_specs, check_vma=False)
```

```python
import functools
import math

import jax
import jax.numpy as jnp
from jax import lax
from jax.experimental import pallas as pl
from jax.experimental.pallas import tpu as pltpu
from jax.sharding import PartitionSpec as P

BLK = 128
TILE = 256
DOCS = 32
DEPTH = 8
HALVES = 2
PARTS = 4
AHEAD = 6

NT = (((1,), (1,)), ((), ()))
TN = (((0,), (0,)), ((), ()))


def flat(block):
    return block.reshape(block.shape[0] * block.shape[1], block.shape[2])


def columns_of(refs, at, count):
    return jnp.concatenate([flat(ref[pl.ds(at, count)]) for ref in refs], axis=1)


def gram_dot(left, right):
    return lax.dot_general(left, right, NT, preferred_element_type=jnp.float32)


def places():
    spot = lax.broadcasted_iota(jnp.int32, (TILE, TILE), 0)
    column = lax.broadcasted_iota(jnp.int32, (TILE, TILE), 1)
    return spot, column


def pair_products(old, own):
    spot, column = places()
    return jnp.where(spot <= column, gram_dot(own, own), gram_dot(old, own))


def counted(pairs, first):
    spot, column = places()
    weight = jnp.where(spot == column, jnp.float32(1.0), jnp.float32(2.0))
    begin = jnp.where(spot <= column, first, first + TILE)
    return jnp.where(spot >= begin, pairs * weight, jnp.float32(0.0))


def line_of(ref, at, row):
    line = slice(row, row + 1)
    return jnp.concatenate([ref[at, line], ref[at + 1, line]], axis=1)


def doc_sums(terms, ids):
    docs = lax.broadcasted_iota(jnp.int32, (DOCS, TILE), 0)
    total = jnp.sum(terms, axis=0, keepdims=True)
    parts = jnp.where(docs == ids, jnp.broadcast_to(total, docs.shape), jnp.float32(0.0))
    return parts[:, :BLK] + parts[:, BLK:]


def hidden_kernel(kinds, first_ref, *refs):
    per_row = 2 * HALVES
    out_ref = refs[-1]
    tiles = out_ref.shape[1]
    step = pl.program_id(0)
    for k, row in enumerate(kinds):
        row_refs = refs[per_row * k : per_row * (k + 1)]
        old = columns_of(row_refs[HALVES:], 0, 2)
        for t in range(tiles):
            number = step * tiles + t
            first = line_of(first_ref, 2 * number, row) - number * TILE
            own = columns_of(row_refs[:HALVES], 2 * t, 2)
            out_ref[k, t] = counted(pair_products(old, own), first)
            old = own


def hidden_gram(first, kinds, hidden, total, into=None):
    pieces = [piece for row in hidden for piece in row]
    blocks = pieces[0].shape[0]
    count = blocks // PARTS
    tiles = count // 2
    nrows = len(kinds)
    own = pl.BlockSpec((count, BLK, BLK), lambda i: (i, 0, 0))
    old = pl.BlockSpec((2, BLK, BLK), lambda i: (jnp.maximum(i * tiles - 1, 0), 0, 0))
    place = kinds[0] // nrows
    operands = [first, *[piece for row in hidden for piece in [*row, *row]]]
    specs = [
        pl.BlockSpec(first.shape, lambda i: (0, 0, 0)),
        *[spec for _ in kinds for spec in [own] * HALVES + [old] * HALVES],
    ]
    aliases = {}
    if into is not None:
        aliases = {len(operands): 0}
        operands.append(keep_in(pltpu.HBM, into))
        specs.append(pl.BlockSpec(memory_space=pltpu.HBM))
    return pl.pallas_call(
        functools.partial(hidden_kernel, kinds),
        out_shape=pltpu.HBM((total, blocks // 2, TILE, TILE), jnp.float32),
        grid=(PARTS,),
        in_specs=specs,
        out_specs=pl.BlockSpec((nrows, tiles, TILE, TILE), lambda i: (place, i, 0, 0)),
        input_output_aliases=aliases,
        compiler_params=pltpu.CompilerParams(vmem_limit_bytes=24 * 2**20),
        cost_estimate=pl.CostEstimate(
            flops=nrows * blocks * BLK * 4 * TILE * TILE,
            bytes_accessed=nrows * blocks * BLK * TILE * 6,
            transcendentals=0,
        ),
        name="hidden_gram",
    )(*operands)


def early_kernel(kinds, rows_ref, ids_ref, pairs_hbm, g_hbm, out_ref, g_ref, last_ref, pairs_ref, pair_sems, sems):
    nrows = len(kinds)
    blocks, every = g_ref.shape[:2]
    count = blocks // PARTS
    tiles = count // 2

    def copy(n):
        here = pl.ds(lax.rem(n, PARTS) * count, count)
        row = n // PARTS
        return pltpu.make_async_copy(g_hbm.at[here, row], g_ref.at[here, row], sems.at[n])

    def pair_copy(n):
        here = pl.ds(lax.rem(n, PARTS) * tiles, tiles)
        slot = lax.rem(n, AHEAD + 2)
        return pltpu.make_async_copy(pairs_hbm.at[n // PARTS, here], pairs_ref.at[slot], pair_sems.at[n])

    for n in range(AHEAD):
        copy(n).start()
        pair_copy(n).start()
    out_ref[...] = jnp.zeros_like(out_ref)

    def add(k, row, c, parts):
        for n in (k * PARTS + c + p for p in range(parts)):
            copy(n).wait()
            pair_copy(n).wait()

            @pl.when(n + AHEAD < every * PARTS)
            def _():
                copy(n + AHEAD).start()

            @pl.when(n + AHEAD < nrows * PARTS)
            def _():
                pair_copy(n + AHEAD).start()

        share = jnp.zeros((DOCS, BLK), jnp.float32)
        begin = c * count
        old = flat(g_ref[pl.ds(jnp.maximum(begin - 2, 0), 2), row])
        for t in range(parts * tiles):
            at = begin + 2 * t
            slot = lax.rem(k * PARTS + c + t // tiles, AHEAD + 2)
            own = flat(g_ref[pl.ds(at, 2), row])
            terms = pairs_ref[slot, t % tiles] * pair_products(old, own)
            share += doc_sums(terms, line_of(ids_ref, at, row))
            old = own
        here = pl.ds(pl.multiple_of(rows_ref[row] * DOCS, DOCS), DOCS)
        out_ref[here, :] += share

    for k, row in enumerate(kinds):
        if k == 0:
            pl.loop(0, 2)(lambda c, k=k, row=row: add(k, row, c, 1))
            add(k, row, 2, PARTS - 2)
        else:
            pl.loop(0, PARTS // 2)(lambda i, k=k, row=row: add(k, row, 2 * i, 2))

    @pl.loop(0, PARTS // 2)
    def _(i):
        for n in (nrows * PARTS + 2 * i, nrows * PARTS + 2 * i + 1):
            copy(n).wait()
        begin = 2 * i * count
        old = flat(g_ref[pl.ds(jnp.maximum(begin - 2, 0), 2), nrows])
        for t in range(2 * tiles):
            own = flat(g_ref[pl.ds(begin + 2 * t, 2), nrows])
            last_ref[2 * i * tiles + t] = pair_products(old, own)
            old = own


def late_kernel(row, rows_ref, ids_ref, first_ref, *refs):
    pieces = refs[:HALVES]
    last_ref, init_ref, out_ref, acc, h_ref, sems = refs[HALVES:]
    count = h_ref.shape[1] // PARTS
    tiles = count // 2

    def copies(c):
        here = pl.ds(c * count, count)
        return [
            pltpu.make_async_copy(piece.at[here], h_ref.at[q, here], sems.at[c, q])
            for q, piece in enumerate(pieces)
        ]

    for c in range(PARTS):
        for copy in copies(c):
            copy.start()
    acc[...] = init_ref[...]
    h_refs = [h_ref.at[q] for q in range(HALVES)]
    share = jnp.zeros((DOCS, BLK), jnp.float32)
    for c in range(PARTS):
        for copy in copies(c):
            copy.wait()
        old = columns_of(h_refs, max(c * count - 2, 0), 2)
        for t in range(tiles):
            number = c * tiles + t
            first = line_of(first_ref, 2 * number, row) - number * TILE
            own = columns_of(h_refs, 2 * number, 2)
            terms = counted(pair_products(old, own), first) * last_ref[number]
            share += doc_sums(terms, line_of(ids_ref, 2 * number, row))
            old = own
    here = pl.ds(pl.multiple_of(rows_ref[row] * DOCS, DOCS), DOCS)
    acc[here, :] += share

    sums = jnp.sum(acc[...].T, axis=0, keepdims=True)
    out_ref[...] = jnp.broadcast_to(sums[None], out_ref.shape)


def in_vmem(count):
    return [pl.BlockSpec(memory_space=pltpu.VMEM)] * count


def in_hbm(count):
    return [pl.BlockSpec(memory_space=pltpu.HBM)] * count


def keep_in(space, array):
    return pltpu.with_memory_space_constraint(array, space)


def gram_cost(nrows, grad):
    blocks, _, _, width = grad.shape
    return pl.CostEstimate(
        flops=nrows * blocks * BLK * 4 * TILE * (TILE + width),
        bytes_accessed=grad.size * 2,
        transcendentals=0,
    )


def gram_early(rows, ids, kinds, pairs, grad):
    every = grad.shape[1]
    tiles = pairs.shape[1] // PARTS
    return pl.pallas_call(
        functools.partial(early_kernel, kinds),
        out_shape=[
            jax.ShapeDtypeStruct((every * DOCS, BLK), jnp.float32),
            pltpu.VMEM(grad.shape, grad.dtype),
            pltpu.VMEM((pairs.shape[1], TILE, TILE), jnp.float32),
        ],
        grid_spec=pltpu.PrefetchScalarGridSpec(
            num_scalar_prefetch=1,
            grid=(),
            in_specs=[*in_vmem(1), *in_hbm(2)],
            out_specs=in_vmem(3),
            scratch_shapes=[
                pltpu.VMEM((AHEAD + 2, tiles, TILE, TILE), jnp.float32),
                pltpu.SemaphoreType.DMA((len(kinds) * PARTS,)),
                pltpu.SemaphoreType.DMA((every * PARTS,)),
            ],
        ),
        compiler_params=pltpu.CompilerParams(vmem_limit_bytes=12 * 2**20),
        cost_estimate=gram_cost(len(kinds), grad),
        name="gram",
    )(rows, ids, keep_in(pltpu.HBM, pairs), keep_in(pltpu.HBM, grad))


def gram_late(rows, ids, first, row, hidden, last, init, devices):
    return pl.pallas_call(
        functools.partial(late_kernel, row),
        out_shape=jax.ShapeDtypeStruct((devices, 1, BLK), jnp.float32),
        grid_spec=pltpu.PrefetchScalarGridSpec(
            num_scalar_prefetch=1,
            grid=(),
            in_specs=[*in_vmem(2), *in_hbm(len(hidden)), *in_vmem(2)],
            out_specs=pl.BlockSpec(memory_space=pltpu.VMEM),
            scratch_shapes=[
                pltpu.VMEM(init.shape, jnp.float32),
                pltpu.VMEM((len(hidden), *hidden[0].shape), hidden[0].dtype),
                pltpu.SemaphoreType.DMA((PARTS, len(hidden))),
            ],
        ),
        compiler_params=pltpu.CompilerParams(vmem_limit_bytes=8 * 2**20),
        cost_estimate=pl.CostEstimate(
            flops=2 * 2 * last.size * TILE, bytes_accessed=last.size * 4, transcendentals=0
        ),
        name="gram_late",
    )(rows, ids, first, *hidden, keep_in(pltpu.VMEM, last), init)


def product_kernel(nrows, bound, rows_ref, ids_ref, norms_ref, *refs):
    pieces = refs[: HALVES * nrows]
    g_ref, out_ref, h_ref, h_sems, factor, scaled = refs[HALVES * nrows :]
    blocks = g_ref.shape[0]
    steps = blocks // DEPTH

    order = [nrows - 2, *range(nrows - 2), nrows - 1]

    def hidden_copies(k):
        return [
            pltpu.make_async_copy(pieces[n], h_ref.at[n], h_sems.at[n])
            for n in range(HALVES * k, HALVES * (k + 1))
        ]

    for piece in hidden_copies(order[0]):
        piece.start()
    norms = jnp.maximum(jnp.sum(norms_ref[...], axis=0), 0.0)
    clip = bound / jnp.maximum(jnp.sqrt(norms), bound) / nrows
    for k in range(nrows):
        ids = ids_ref[:, k, :] + rows_ref[k] * DOCS
        table = jnp.broadcast_to(clip, ids.shape)
        factor[k] = jnp.take_along_axis(table, ids, axis=1)

    def scale(n, slot):
        k, begin = order[n // steps], n % steps * DEPTH
        lines = jnp.concatenate([factor[k, begin : begin + DEPTH, :]] * (BLK // DEPTH), axis=0).T
        for j in range(DEPTH):
            factors = jnp.broadcast_to(lines[:, j : j + 1], (BLK, BLK))
            for c in range(0, g_ref.shape[3], BLK):
                grad = g_ref[begin + j, k, :, c : c + BLK].astype(jnp.float32)
                scaled[slot, j * BLK : (j + 1) * BLK, c : c + BLK] = (grad * factors).astype(jnp.bfloat16)

    scale(0, 0)
    for n in range(nrows * steps):
        k, begin = order[n // steps], n % steps * DEPTH
        if begin == 0:
            for piece in hidden_copies(k):
                piece.wait()
            if n // steps + 1 < nrows:
                for piece in hidden_copies(order[n // steps + 1]):
                    piece.start()
        if n + 1 < nrows * steps:
            scale(n + 1, (n + 1) % 2)
        share = lax.dot_general(
            columns_of([h_ref.at[HALVES * k + q] for q in range(HALVES)], begin, DEPTH),
            scaled[n % 2],
            TN,
            preferred_element_type=jnp.float32,
        )
        if n == 0:
            out_ref[...] = share
        else:
            out_ref[...] += share


def product(rows, ids, norms, hidden, grad, bound):
    blocks, nrows, _, width = grad.shape
    pieces = [piece for row in hidden for piece in row]
    return pl.pallas_call(
        functools.partial(product_kernel, nrows, bound),
        out_shape=pltpu.HBM((TILE, width), jnp.float32),
        grid_spec=pltpu.PrefetchScalarGridSpec(
            num_scalar_prefetch=1,
            grid=(),
            in_specs=[*in_vmem(2), *in_hbm(len(pieces)), *in_vmem(1)],
            out_specs=pl.BlockSpec(memory_space=pltpu.VMEM),
            scratch_shapes=[
                pltpu.VMEM((len(pieces), *pieces[0].shape), grad.dtype),
                pltpu.SemaphoreType.DMA((len(pieces),)),
                pltpu.VMEM((nrows, blocks, BLK), jnp.float32),
                pltpu.VMEM((2, DEPTH * BLK, width), jnp.bfloat16),
            ],
        ),
        compiler_params=pltpu.CompilerParams(vmem_limit_bytes=14 * 2**20),
        cost_estimate=pl.CostEstimate(
            flops=2 * nrows * blocks * BLK * TILE * width,
            bytes_accessed=nrows * blocks * BLK * 2 * (TILE + width),
            transcendentals=0,
        ),
        name="product",
    )(rows, ids, norms, *pieces, keep_in(pltpu.VMEM, grad))


def quarters_kernel(offsets, me_ref, ids_ref, grad_ref, *refs):
    out_refs, sems = refs[:-1], refs[-1]
    tokens = grad_ref.shape[0]
    part = out_refs[0].shape[1]
    count = len(offsets)
    copies = []
    for n, (offset, out_ref) in enumerate(zip(offsets, out_refs)):
        begin = pl.multiple_of(lax.rem(me_ref[0] + offset, count) * part, BLK)
        source = grad_ref.at[:, pl.ds(begin, part)]
        copies.append(pltpu.make_async_copy(source, out_ref.at[pl.ds(0, tokens)], sems.at[n]))
    for copy in copies:
        copy.start()
    ids = jnp.broadcast_to(ids_ref[...].astype(jnp.float32).astype(jnp.bfloat16), (16, BLK))
    for out_ref in out_refs:
        out_ref[tokens:, :BLK] = ids
        out_ref[tokens:, BLK:] = jnp.zeros((16, part - BLK), jnp.bfloat16)
    for copy in copies:
        copy.wait()


def quarters(me, offsets, grad, ids):
    tokens, width = grad.shape
    count = len(offsets)
    return pl.pallas_call(
        functools.partial(quarters_kernel, offsets),
        out_shape=[pltpu.VMEM((tokens + 16, width // count), grad.dtype)] * count,
        grid_spec=pltpu.PrefetchScalarGridSpec(
            num_scalar_prefetch=1,
            grid=(),
            in_specs=[*in_vmem(1), *in_hbm(1)],
            out_specs=in_vmem(count),
            scratch_shapes=[pltpu.SemaphoreType.DMA((count,))],
        ),
        name="quarters",
    )(me, ids, keep_in(pltpu.HBM, grad))


def columns_kernel(in_ref, *out_refs):
    for j in range(out_refs[0].shape[0]):
        for q, out_ref in enumerate(out_refs):
            at = (j * HALVES + q) * BLK
            out_ref[j] = in_ref[:, at : at + BLK]


def columns(hidden, blocks, steps=4):
    tokens, width = hidden.shape
    count = blocks // steps
    return pl.pallas_call(
        columns_kernel,
        out_shape=[jax.ShapeDtypeStruct((blocks, tokens, BLK), hidden.dtype)] * HALVES,
        grid=(steps,),
        in_specs=[pl.BlockSpec((tokens, width // steps), lambda i: (0, i))],
        out_specs=[pl.BlockSpec((count, tokens, BLK), lambda i: (i, 0, 0))] * HALVES,
        name="columns",
    )(hidden)


def shift(block, distance):
    size = lax.axis_size("dp")
    return lax.ppermute(block, "dp", [(i, (i + distance) % size) for i in range(size)])


def starts(ids):
    docs = jnp.arange(DOCS, dtype=jnp.int32)
    before = jnp.sum((ids[None] < docs[:, None, None, None]).astype(jnp.int32), axis=(1, 3))
    own = ids[None] == docs[:, None, None, None]
    return jnp.sum(jnp.where(own, before[:, None, :, None], 0), axis=0)


def body(hidden, grad_out, segment):
    row_count = lax.axis_size("dp")
    blocks = lax.axis_size("ctx")
    tokens, width_hidden = hidden.shape[1:]
    width_grad = grad_out.shape[2]
    me = lax.axis_index("dp")

    keep, up, down, across = quarters(me[None], (0, 1, 3, 2), grad_out[0], segment)
    received = [shift(up, 1), shift(down, -1), keep, shift(across, 2)]

    chunks = columns(hidden[0], blocks)
    def rest(received, chunks):
        received, _ = lax.optimization_barrier((received, chunks))

        every_grad = jnp.stack([part[:tokens] for part in received])
        every_grad = lax.all_gather(every_grad, "ctx", axis=0, tiled=False)

        hidden_rows = [[], [], [], []]
        ready = None
        for q, chunk in enumerate(chunks):
            if ready is not None:
                chunk, ready = lax.optimization_barrier((chunk, ready))
            own = lax.all_to_all(chunk, "ctx", 0, 0, tiled=True)
            ready = own
            below, above = lax.optimization_barrier((shift(own, 1), shift(own, -1)))
            far = shift(below, 1) if q < HALVES // 2 else shift(above, -1)
            for row, piece in zip(hidden_rows, (below, above, own, far)):
                row.append(piece)

        ids = jnp.stack([part[tokens, :BLK] for part in received]).astype(jnp.int32)
        ids, ready = lax.optimization_barrier((ids, ready))
        ids = jnp.broadcast_to(ids[None], (blocks, row_count, tokens))
        ids = lax.all_to_all(ids, "ctx", 0, 0, tiled=True)
        first = starts(ids)

        rows = lax.rem(me + jnp.array([3, 1, 0, 2], jnp.int32), row_count)
        kinds = (0, 1, 2)
        pairs = hidden_gram(first, kinds[2:], hidden_rows[2:3], len(kinds))
        pairs = hidden_gram(first, kinds[:2], hidden_rows[:2], len(kinds), pairs)
        early, grads, last = gram_early(rows, ids, kinds, pairs, every_grad)
        devices = row_count * blocks
        partial = gram_late(rows, ids, first, 3, hidden_rows[3], last, early, devices)
        norms = lax.all_to_all(partial, ("dp", "ctx"), 0, 0, tiled=True)

        bound = math.sqrt(tokens * width_hidden * width_grad)
        return product(rows, ids, norms, hidden_rows, grads, bound)

    nothing = lambda *_: jnp.zeros((TILE, width_grad // row_count), jnp.float32)
    return lax.cond(me < row_count, rest, nothing, received, chunks)


def solution(mesh):
    in_specs = (P("dp", "ctx", None), P("dp", "ctx", None), P("dp", "ctx"))
    out_specs = P("ctx", "dp")
    return jax.shard_map(body, mesh=mesh, in_specs=in_specs, out_specs=out_specs, check_vma=False)
```

```python
import functools
import math

import jax
import jax.numpy as jnp
from jax import lax
from jax.experimental import pallas as pl
from jax.experimental.pallas import tpu as pltpu
from jax.sharding import PartitionSpec as P

BLK = 128
TILE = 256
DOCS = 32
DEPTH = 8
HALVES = 2
PARTS = 4
AHEAD = 6

NT = (((1,), (1,)), ((), ()))
TN = (((0,), (0,)), ((), ()))


def flat(block):
    return block.reshape(block.shape[0] * block.shape[1], block.shape[2])


def columns_of(refs, at, count):
    return jnp.concatenate([flat(ref[pl.ds(at, count)]) for ref in refs], axis=1)


def gram_dot(left, right):
    return lax.dot_general(left, right, NT, preferred_element_type=jnp.float32)


def places():
    spot = lax.broadcasted_iota(jnp.int32, (TILE, TILE), 0)
    column = lax.broadcasted_iota(jnp.int32, (TILE, TILE), 1)
    return spot, column


def pair_products(old, own):
    spot, column = places()
    return jnp.where(spot <= column, gram_dot(own, own), gram_dot(old, own))


def counted(pairs, first):
    spot, column = places()
    weight = jnp.where(spot == column, jnp.float32(1.0), jnp.float32(2.0))
    begin = jnp.where(spot <= column, first, first + TILE)
    return jnp.where(spot >= begin, pairs * weight, jnp.float32(0.0))


def line_of(ref, at, row):
    line = slice(row, row + 1)
    return jnp.concatenate([ref[at, line], ref[at + 1, line]], axis=1)


def doc_sums(terms, ids):
    docs = lax.broadcasted_iota(jnp.int32, (DOCS, TILE), 0)
    total = jnp.sum(terms, axis=0, keepdims=True)
    parts = jnp.where(docs == ids, jnp.broadcast_to(total, docs.shape), jnp.float32(0.0))
    return parts[:, :BLK] + parts[:, BLK:]


def hidden_kernel(kinds, first_ref, *refs):
    per_row = 2 * HALVES
    out_ref = refs[-1]
    tiles = out_ref.shape[1]
    step = pl.program_id(0)
    for k, row in enumerate(kinds):
        row_refs = refs[per_row * k : per_row * (k + 1)]
        old = columns_of(row_refs[HALVES:], 0, 2)
        for t in range(tiles):
            number = step * tiles + t
            first = line_of(first_ref, 2 * number, row) - number * TILE
            own = columns_of(row_refs[:HALVES], 2 * t, 2)
            out_ref[k, t] = counted(pair_products(old, own), first)
            old = own


def hidden_gram(first, kinds, hidden, total, into=None):
    pieces = [piece for row in hidden for piece in row]
    blocks = pieces[0].shape[0]
    count = blocks // PARTS
    tiles = count // 2
    nrows = len(kinds)
    own = pl.BlockSpec((count, BLK, BLK), lambda i: (i, 0, 0))
    old = pl.BlockSpec((2, BLK, BLK), lambda i: (jnp.maximum(i * tiles - 1, 0), 0, 0))
    place = kinds[0] // nrows
    operands = [first, *[piece for row in hidden for piece in [*row, *row]]]
    specs = [
        pl.BlockSpec(first.shape, lambda i: (0, 0, 0)),
        *[spec for _ in kinds for spec in [own] * HALVES + [old] * HALVES],
    ]
    aliases = {}
    if into is not None:
        aliases = {len(operands): 0}
        operands.append(keep_in(pltpu.HBM, into))
        specs.append(pl.BlockSpec(memory_space=pltpu.HBM))
    return pl.pallas_call(
        functools.partial(hidden_kernel, kinds),
        out_shape=pltpu.HBM((total, blocks // 2, TILE, TILE), jnp.float32),
        grid=(PARTS,),
        in_specs=specs,
        out_specs=pl.BlockSpec((nrows, tiles, TILE, TILE), lambda i: (place, i, 0, 0)),
        input_output_aliases=aliases,
        compiler_params=pltpu.CompilerParams(vmem_limit_bytes=24 * 2**20),
        cost_estimate=pl.CostEstimate(
            flops=nrows * blocks * BLK * 4 * TILE * TILE,
            bytes_accessed=nrows * blocks * BLK * TILE * 6,
            transcendentals=0,
        ),
        name="hidden_gram",
    )(*operands)


def early_kernel(kinds, rows_ref, ids_ref, first_ref, pairs_hbm, g_hbm, out_ref, g_ref, last_ref, pairs_ref, pair_sems, sems):
    nrows = len(kinds)
    blocks, every = g_ref.shape[:2]
    count = blocks // PARTS
    tiles = count // 2

    def copy(n):
        here = pl.ds(lax.rem(n, PARTS) * count, count)
        row = n // PARTS
        return pltpu.make_async_copy(g_hbm.at[here, row], g_ref.at[here, row], sems.at[n])

    def pair_copy(n):
        here = pl.ds(lax.rem(n, PARTS) * tiles, tiles)
        slot = lax.rem(n, AHEAD + 2)
        return pltpu.make_async_copy(pairs_hbm.at[n // PARTS, here], pairs_ref.at[slot], pair_sems.at[n])

    for n in range(AHEAD):
        copy(n).start()
        pair_copy(n).start()
    out_ref[...] = jnp.zeros_like(out_ref)

    def add(k, row, c, parts):
        for n in (k * PARTS + c + p for p in range(parts)):
            copy(n).wait()
            pair_copy(n).wait()

            @pl.when(n + AHEAD < every * PARTS)
            def _():
                copy(n + AHEAD).start()

            @pl.when(n + AHEAD < nrows * PARTS)
            def _():
                pair_copy(n + AHEAD).start()

        share = jnp.zeros((DOCS, BLK), jnp.float32)
        begin = c * count
        old = flat(g_ref[pl.ds(jnp.maximum(begin - 2, 0), 2), row])
        for t in range(parts * tiles):
            at = begin + 2 * t
            slot = lax.rem(k * PARTS + c + t // tiles, AHEAD + 2)
            own = flat(g_ref[pl.ds(at, 2), row])
            terms = pairs_ref[slot, t % tiles] * pair_products(old, own)
            share += doc_sums(terms, line_of(ids_ref, at, row))
            old = own
        here = pl.ds(pl.multiple_of(rows_ref[row] * DOCS, DOCS), DOCS)
        out_ref[here, :] += share

    for k, row in enumerate(kinds):
        if k == 0:
            pl.loop(0, 2)(lambda c, k=k, row=row: add(k, row, c, 1))
            add(k, row, 2, PARTS - 2)
        else:
            pl.loop(0, PARTS // 2)(lambda i, k=k, row=row: add(k, row, 2 * i, 2))

    @pl.loop(0, PARTS // 2)
    def _(i):
        for n in (nrows * PARTS + 2 * i, nrows * PARTS + 2 * i + 1):
            copy(n).wait()
        begin = 2 * i * count
        old = flat(g_ref[pl.ds(jnp.maximum(begin - 2, 0), 2), nrows])
        for t in range(2 * tiles):
            own = flat(g_ref[pl.ds(begin + 2 * t, 2), nrows])
            number = 2 * i * tiles + t
            first = line_of(first_ref, 2 * number, nrows) - number * TILE
            last_ref[number] = counted(pair_products(old, own), first)
            old = own


def late_kernel(row, rows_ref, ids_ref, *refs):
    pieces = refs[:HALVES]
    last_ref, init_ref, out_ref, acc, h_ref, sems = refs[HALVES:]
    count = h_ref.shape[1] // PARTS
    tiles = count // 2

    def copies(c):
        here = pl.ds(c * count, count)
        return [
            pltpu.make_async_copy(piece.at[here], h_ref.at[q, here], sems.at[c, q])
            for q, piece in enumerate(pieces)
        ]

    for c in range(PARTS):
        for copy in copies(c):
            copy.start()
    acc[...] = init_ref[...]
    h_refs = [h_ref.at[q] for q in range(HALVES)]
    share = jnp.zeros((DOCS, BLK), jnp.float32)
    for c in range(PARTS):
        for copy in copies(c):
            copy.wait()
        old = columns_of(h_refs, max(c * count - 2, 0), 2)
        for t in range(tiles):
            number = c * tiles + t
            own = columns_of(h_refs, 2 * number, 2)
            terms = pair_products(old, own) * last_ref[number]
            share += doc_sums(terms, line_of(ids_ref, 2 * number, row))
            old = own
    here = pl.ds(pl.multiple_of(rows_ref[row] * DOCS, DOCS), DOCS)
    acc[here, :] += share

    sums = jnp.sum(acc[...].T, axis=0, keepdims=True)
    out_ref[...] = jnp.broadcast_to(sums[None], out_ref.shape)


def in_vmem(count):
    return [pl.BlockSpec(memory_space=pltpu.VMEM)] * count


def in_hbm(count):
    return [pl.BlockSpec(memory_space=pltpu.HBM)] * count


def keep_in(space, array):
    return pltpu.with_memory_space_constraint(array, space)


def gram_cost(nrows, grad):
    blocks, _, _, width = grad.shape
    return pl.CostEstimate(
        flops=nrows * blocks * BLK * 4 * TILE * (TILE + width),
        bytes_accessed=grad.size * 2,
        transcendentals=0,
    )


def gram_early(rows, ids, first, kinds, pairs, grad):
    every = grad.shape[1]
    tiles = pairs.shape[1] // PARTS
    return pl.pallas_call(
        functools.partial(early_kernel, kinds),
        out_shape=[
            jax.ShapeDtypeStruct((every * DOCS, BLK), jnp.float32),
            pltpu.VMEM(grad.shape, grad.dtype),
            pltpu.VMEM((pairs.shape[1], TILE, TILE), jnp.float32),
        ],
        grid_spec=pltpu.PrefetchScalarGridSpec(
            num_scalar_prefetch=1,
            grid=(),
            in_specs=[*in_vmem(2), *in_hbm(2)],
            out_specs=in_vmem(3),
            scratch_shapes=[
                pltpu.VMEM((AHEAD + 2, tiles, TILE, TILE), jnp.float32),
                pltpu.SemaphoreType.DMA((len(kinds) * PARTS,)),
                pltpu.SemaphoreType.DMA((every * PARTS,)),
            ],
        ),
        compiler_params=pltpu.CompilerParams(vmem_limit_bytes=12 * 2**20),
        cost_estimate=gram_cost(len(kinds), grad),
        name="gram",
    )(rows, ids, first, keep_in(pltpu.HBM, pairs), keep_in(pltpu.HBM, grad))


def gram_late(rows, ids, row, hidden, last, init, devices):
    return pl.pallas_call(
        functools.partial(late_kernel, row),
        out_shape=jax.ShapeDtypeStruct((devices, 1, BLK), jnp.float32),
        grid_spec=pltpu.PrefetchScalarGridSpec(
            num_scalar_prefetch=1,
            grid=(),
            in_specs=[*in_vmem(1), *in_hbm(len(hidden)), *in_vmem(2)],
            out_specs=pl.BlockSpec(memory_space=pltpu.VMEM),
            scratch_shapes=[
                pltpu.VMEM(init.shape, jnp.float32),
                pltpu.VMEM((len(hidden), *hidden[0].shape), hidden[0].dtype),
                pltpu.SemaphoreType.DMA((PARTS, len(hidden))),
            ],
        ),
        compiler_params=pltpu.CompilerParams(vmem_limit_bytes=8 * 2**20),
        cost_estimate=pl.CostEstimate(
            flops=2 * 2 * last.size * TILE, bytes_accessed=last.size * 4, transcendentals=0
        ),
        name="gram_late",
    )(rows, ids, *hidden, keep_in(pltpu.VMEM, last), init)


def product_kernel(nrows, bound, rows_ref, ids_ref, norms_ref, *refs):
    pieces = refs[: HALVES * nrows]
    g_ref, out_ref, h_ref, h_sems, factor, scaled = refs[HALVES * nrows :]
    blocks = g_ref.shape[0]
    steps = blocks // DEPTH

    order = [nrows - 2, *range(nrows - 2), nrows - 1]

    def hidden_copies(k):
        return [
            pltpu.make_async_copy(pieces[n], h_ref.at[n], h_sems.at[n])
            for n in range(HALVES * k, HALVES * (k + 1))
        ]

    for piece in hidden_copies(order[0]):
        piece.start()
    norms = jnp.maximum(jnp.sum(norms_ref[...], axis=0), 0.0)
    clip = bound / jnp.maximum(jnp.sqrt(norms), bound) / nrows
    for k in range(nrows):
        ids = ids_ref[:, k, :] + rows_ref[k] * DOCS
        table = jnp.broadcast_to(clip, ids.shape)
        factor[k] = jnp.take_along_axis(table, ids, axis=1)

    def scale(n, slot):
        k, begin = order[n // steps], n % steps * DEPTH
        lines = jnp.concatenate([factor[k, begin : begin + DEPTH, :]] * (BLK // DEPTH), axis=0).T
        for j in range(DEPTH):
            factors = jnp.broadcast_to(lines[:, j : j + 1], (BLK, BLK))
            for c in range(0, g_ref.shape[3], BLK):
                grad = g_ref[begin + j, k, :, c : c + BLK].astype(jnp.float32)
                scaled[slot, j * BLK : (j + 1) * BLK, c : c + BLK] = (grad * factors).astype(jnp.bfloat16)

    scale(0, 0)
    for n in range(nrows * steps):
        k, begin = order[n // steps], n % steps * DEPTH
        if begin == 0:
            for piece in hidden_copies(k):
                piece.wait()
            if n // steps + 1 < nrows:
                for piece in hidden_copies(order[n // steps + 1]):
                    piece.start()
        if n + 1 < nrows * steps:
            scale(n + 1, (n + 1) % 2)
        share = lax.dot_general(
            columns_of([h_ref.at[HALVES * k + q] for q in range(HALVES)], begin, DEPTH),
            scaled[n % 2],
            TN,
            preferred_element_type=jnp.float32,
        )
        if n == 0:
            out_ref[...] = share
        else:
            out_ref[...] += share


def product(rows, ids, norms, hidden, grad, bound):
    blocks, nrows, _, width = grad.shape
    pieces = [piece for row in hidden for piece in row]
    return pl.pallas_call(
        functools.partial(product_kernel, nrows, bound),
        out_shape=pltpu.HBM((TILE, width), jnp.float32),
        grid_spec=pltpu.PrefetchScalarGridSpec(
            num_scalar_prefetch=1,
            grid=(),
            in_specs=[*in_vmem(2), *in_hbm(len(pieces)), *in_vmem(1)],
            out_specs=pl.BlockSpec(memory_space=pltpu.VMEM),
            scratch_shapes=[
                pltpu.VMEM((len(pieces), *pieces[0].shape), grad.dtype),
                pltpu.SemaphoreType.DMA((len(pieces),)),
                pltpu.VMEM((nrows, blocks, BLK), jnp.float32),
                pltpu.VMEM((2, DEPTH * BLK, width), jnp.bfloat16),
            ],
        ),
        compiler_params=pltpu.CompilerParams(vmem_limit_bytes=14 * 2**20),
        cost_estimate=pl.CostEstimate(
            flops=2 * nrows * blocks * BLK * TILE * width,
            bytes_accessed=nrows * blocks * BLK * 2 * (TILE + width),
            transcendentals=0,
        ),
        name="product",
    )(rows, ids, norms, *pieces, keep_in(pltpu.VMEM, grad))


def quarters_kernel(offsets, me_ref, ids_ref, grad_ref, *refs):
    out_refs, sems = refs[:-1], refs[-1]
    tokens = grad_ref.shape[0]
    part = out_refs[0].shape[1]
    count = len(offsets)
    copies = []
    for n, (offset, out_ref) in enumerate(zip(offsets, out_refs)):
        begin = pl.multiple_of(lax.rem(me_ref[0] + offset, count) * part, BLK)
        source = grad_ref.at[:, pl.ds(begin, part)]
        copies.append(pltpu.make_async_copy(source, out_ref.at[pl.ds(0, tokens)], sems.at[n]))
    for copy in copies:
        copy.start()
    ids = jnp.broadcast_to(ids_ref[...].astype(jnp.float32).astype(jnp.bfloat16), (16, BLK))
    for out_ref in out_refs:
        out_ref[tokens:, :BLK] = ids
        out_ref[tokens:, BLK:] = jnp.zeros((16, part - BLK), jnp.bfloat16)
    for copy in copies:
        copy.wait()


def quarters(me, offsets, grad, ids):
    tokens, width = grad.shape
    count = len(offsets)
    return pl.pallas_call(
        functools.partial(quarters_kernel, offsets),
        out_shape=[pltpu.VMEM((tokens + 16, width // count), grad.dtype)] * count,
        grid_spec=pltpu.PrefetchScalarGridSpec(
            num_scalar_prefetch=1,
            grid=(),
            in_specs=[*in_vmem(1), *in_hbm(1)],
            out_specs=in_vmem(count),
            scratch_shapes=[pltpu.SemaphoreType.DMA((count,))],
        ),
        name="quarters",
    )(me, ids, keep_in(pltpu.HBM, grad))


def columns_kernel(in_ref, *out_refs):
    for j in range(out_refs[0].shape[0]):
        for q, out_ref in enumerate(out_refs):
            at = (j * HALVES + q) * BLK
            out_ref[j] = in_ref[:, at : at + BLK]


def columns(hidden, blocks, steps=4):
    tokens, width = hidden.shape
    count = blocks // steps
    return pl.pallas_call(
        columns_kernel,
        out_shape=[jax.ShapeDtypeStruct((blocks, tokens, BLK), hidden.dtype)] * HALVES,
        grid=(steps,),
        in_specs=[pl.BlockSpec((tokens, width // steps), lambda i: (0, i))],
        out_specs=[pl.BlockSpec((count, tokens, BLK), lambda i: (i, 0, 0))] * HALVES,
        name="columns",
    )(hidden)


def shift(block, distance):
    size = lax.axis_size("dp")
    return lax.ppermute(block, "dp", [(i, (i + distance) % size) for i in range(size)])


def starts(ids):
    docs = jnp.arange(DOCS, dtype=jnp.int32)
    before = jnp.sum((ids[None] < docs[:, None, None, None]).astype(jnp.int32), axis=(1, 3))
    own = ids[None] == docs[:, None, None, None]
    return jnp.sum(jnp.where(own, before[:, None, :, None], 0), axis=0)


def body(hidden, grad_out, segment):
    row_count = lax.axis_size("dp")
    blocks = lax.axis_size("ctx")
    tokens, width_hidden = hidden.shape[1:]
    width_grad = grad_out.shape[2]
    me = lax.axis_index("dp")

    keep, up, down, across = quarters(me[None], (0, 1, 3, 2), grad_out[0], segment)
    received = [shift(up, 1), shift(down, -1), keep, shift(across, 2)]

    chunks = columns(hidden[0], blocks)
    def rest(received, chunks):
        received, _ = lax.optimization_barrier((received, chunks))

        every_grad = jnp.stack([part[:tokens] for part in received])
        every_grad = lax.all_gather(every_grad, "ctx", axis=0, tiled=False)

        hidden_rows = [[], [], [], []]
        ready = None
        for q, chunk in enumerate(chunks):
            if ready is not None:
                chunk, ready = lax.optimization_barrier((chunk, ready))
            own = lax.all_to_all(chunk, "ctx", 0, 0, tiled=True)
            ready = own
            below, above = lax.optimization_barrier((shift(own, 1), shift(own, -1)))
            far = shift(below, 1) if q < HALVES // 2 else shift(above, -1)
            for row, piece in zip(hidden_rows, (below, above, own, far)):
                row.append(piece)

        ids = jnp.stack([part[tokens, :BLK] for part in received]).astype(jnp.int32)
        ids, ready = lax.optimization_barrier((ids, ready))
        ids = jnp.broadcast_to(ids[None], (blocks, row_count, tokens))
        ids = lax.all_to_all(ids, "ctx", 0, 0, tiled=True)
        first = starts(ids)

        rows = lax.rem(me + jnp.array([3, 1, 0, 2], jnp.int32), row_count)
        kinds = (0, 1, 2)
        pairs = hidden_gram(first, kinds[2:], hidden_rows[2:3], len(kinds))
        pairs = hidden_gram(first, kinds[:2], hidden_rows[:2], len(kinds), pairs)
        early, grads, last = gram_early(rows, ids, first, kinds, pairs, every_grad)
        devices = row_count * blocks
        partial = gram_late(rows, ids, 3, hidden_rows[3], last, early, devices)
        norms = lax.all_to_all(partial, ("dp", "ctx"), 0, 0, tiled=True)

        bound = math.sqrt(tokens * width_hidden * width_grad)
        return product(rows, ids, norms, hidden_rows, grads, bound)

    nothing = lambda *_: jnp.zeros((TILE, width_grad // row_count), jnp.float32)
    return lax.cond(me < row_count, rest, nothing, received, chunks)


def solution(mesh):
    in_specs = (P("dp", "ctx", None), P("dp", "ctx", None), P("dp", "ctx"))
    out_specs = P("ctx", "dp")
    return jax.shard_map(body, mesh=mesh, in_specs=in_specs, out_specs=out_specs, check_vma=False)
```

```python
import functools
import math

import jax
import jax.numpy as jnp
from jax import lax
from jax.experimental import pallas as pl
from jax.experimental.pallas import tpu as pltpu
from jax.sharding import PartitionSpec as P

BLK = 128
TILE = 256
DOCS = 32
DEPTH = 8
HALVES = 2
PARTS = 4
AHEAD = 6

NT = (((1,), (1,)), ((), ()))
TN = (((0,), (0,)), ((), ()))


def flat(block):
    return block.reshape(block.shape[0] * block.shape[1], block.shape[2])


def columns_of(refs, at, count):
    return jnp.concatenate([flat(ref[pl.ds(at, count)]) for ref in refs], axis=1)


def gram_dot(left, right):
    return lax.dot_general(left, right, NT, preferred_element_type=jnp.float32)


def places():
    spot = lax.broadcasted_iota(jnp.int32, (TILE, TILE), 0)
    column = lax.broadcasted_iota(jnp.int32, (TILE, TILE), 1)
    return spot, column


def pair_products(old, own):
    spot, column = places()
    return jnp.where(spot <= column, gram_dot(own, own), gram_dot(old, own))


def counted(pairs, first):
    spot, column = places()
    weight = jnp.where(spot == column, jnp.float32(1.0), jnp.float32(2.0))
    begin = jnp.where(spot <= column, first, first + TILE)
    return jnp.where(spot >= begin, pairs * weight, jnp.float32(0.0))


def line_of(ref, at, row):
    line = slice(row, row + 1)
    return jnp.concatenate([ref[at, line], ref[at + 1, line]], axis=1)


def doc_sums(terms, ids):
    docs = lax.broadcasted_iota(jnp.int32, (DOCS, TILE), 0)
    total = jnp.sum(terms, axis=0, keepdims=True)
    parts = jnp.where(docs == ids, jnp.broadcast_to(total, docs.shape), jnp.float32(0.0))
    return parts[:, :BLK] + parts[:, BLK:]


def hidden_kernel(kinds, first_ref, *refs):
    per_row = 2 * HALVES
    out_ref = refs[-1]
    tiles = out_ref.shape[1]
    step = pl.program_id(0)
    for k, row in enumerate(kinds):
        row_refs = refs[per_row * k : per_row * (k + 1)]
        old = columns_of(row_refs[HALVES:], 0, 2)
        for t in range(tiles):
            number = step * tiles + t
            first = line_of(first_ref, 2 * number, row) - number * TILE
            own = columns_of(row_refs[:HALVES], 2 * t, 2)
            out_ref[k, t] = counted(pair_products(old, own), first)
            old = own


def hidden_gram(first, kinds, hidden, total, into=None):
    pieces = [piece for row in hidden for piece in row]
    blocks = pieces[0].shape[0]
    count = blocks // PARTS
    tiles = count // 2
    nrows = len(kinds)
    own = pl.BlockSpec((count, BLK, BLK), lambda i: (i, 0, 0))
    old = pl.BlockSpec((2, BLK, BLK), lambda i: (jnp.maximum(i * tiles - 1, 0), 0, 0))
    place = kinds[0] // nrows
    operands = [first, *[piece for row in hidden for piece in [*row, *row]]]
    specs = [
        pl.BlockSpec(first.shape, lambda i: (0, 0, 0)),
        *[spec for _ in kinds for spec in [own] * HALVES + [old] * HALVES],
    ]
    aliases = {}
    if into is not None:
        aliases = {len(operands): 0}
        operands.append(keep_in(pltpu.HBM, into))
        specs.append(pl.BlockSpec(memory_space=pltpu.HBM))
    return pl.pallas_call(
        functools.partial(hidden_kernel, kinds),
        out_shape=pltpu.HBM((total, blocks // 2, TILE, TILE), jnp.float32),
        grid=(PARTS,),
        in_specs=specs,
        out_specs=pl.BlockSpec((nrows, tiles, TILE, TILE), lambda i: (place, i, 0, 0)),
        input_output_aliases=aliases,
        compiler_params=pltpu.CompilerParams(vmem_limit_bytes=24 * 2**20),
        cost_estimate=pl.CostEstimate(
            flops=nrows * blocks * BLK * 4 * TILE * TILE,
            bytes_accessed=nrows * blocks * BLK * TILE * 6,
            transcendentals=0,
        ),
        name="hidden_gram",
    )(*operands)


def early_kernel(kinds, rows_ref, ids_ref, pairs_hbm, g_hbm, out_ref, g_ref, last_ref, pairs_ref, pair_sems, sems):
    nrows = len(kinds)
    blocks, every = g_ref.shape[:2]
    count = blocks // PARTS
    tiles = count // 2

    def copy(n):
        here = pl.ds(lax.rem(n, PARTS) * count, count)
        row = n // PARTS
        return pltpu.make_async_copy(g_hbm.at[here, row], g_ref.at[here, row], sems.at[n])

    def pair_copy(n):
        here = pl.ds(lax.rem(n, PARTS) * tiles, tiles)
        slot = lax.rem(n, AHEAD + 2)
        return pltpu.make_async_copy(pairs_hbm.at[n // PARTS, here], pairs_ref.at[slot], pair_sems.at[n])

    for n in range(AHEAD):
        copy(n).start()
        pair_copy(n).start()
    out_ref[...] = jnp.zeros_like(out_ref)

    def add(k, row, c, parts):
        for n in (k * PARTS + c + p for p in range(parts)):
            copy(n).wait()
            pair_copy(n).wait()

            @pl.when(n + AHEAD < every * PARTS)
            def _():
                copy(n + AHEAD).start()

            @pl.when(n + AHEAD < nrows * PARTS)
            def _():
                pair_copy(n + AHEAD).start()

        share = jnp.zeros((DOCS, BLK), jnp.float32)
        begin = c * count
        old = flat(g_ref[pl.ds(jnp.maximum(begin - 2, 0), 2), row])
        for t in range(parts * tiles):
            at = begin + 2 * t
            slot = lax.rem(k * PARTS + c + t // tiles, AHEAD + 2)
            own = flat(g_ref[pl.ds(at, 2), row])
            terms = pairs_ref[slot, t % tiles] * pair_products(old, own)
            share += doc_sums(terms, line_of(ids_ref, at, row))
            old = own
        here = pl.ds(pl.multiple_of(rows_ref[row] * DOCS, DOCS), DOCS)
        out_ref[here, :] += share

    for k, row in enumerate(kinds):
        if k == 0:
            pl.loop(0, 2)(lambda c, k=k, row=row: add(k, row, c, 1))
            add(k, row, 2, PARTS - 2)
        else:
            pl.loop(0, PARTS // 2)(lambda i, k=k, row=row: add(k, row, 2 * i, 2))

    @pl.loop(0, PARTS // 2)
    def _(i):
        for n in (nrows * PARTS + 2 * i, nrows * PARTS + 2 * i + 1):
            copy(n).wait()
        begin = 2 * i * count
        old = flat(g_ref[pl.ds(jnp.maximum(begin - 2, 0), 2), nrows])
        for t in range(2 * tiles):
            own = flat(g_ref[pl.ds(begin + 2 * t, 2), nrows])
            last_ref[2 * i * tiles + t] = pair_products(old, own)
            old = own


def late_kernel(row, rows_ref, ids_ref, first_ref, *refs):
    pieces = refs[:HALVES]
    last_ref, init_ref, out_ref, acc, h_ref, sems = refs[HALVES:]
    count = h_ref.shape[1] // PARTS
    tiles = count // 2

    def copies(c):
        here = pl.ds(c * count, count)
        return [
            pltpu.make_async_copy(piece.at[here], h_ref.at[q, here], sems.at[c, q])
            for q, piece in enumerate(pieces)
        ]

    for c in range(PARTS):
        for copy in copies(c):
            copy.start()
    acc[...] = init_ref[...]
    h_refs = [h_ref.at[q] for q in range(HALVES)]
    share = jnp.zeros((DOCS, BLK), jnp.float32)
    for c in range(PARTS):
        for copy in copies(c):
            copy.wait()
        old = columns_of(h_refs, max(c * count - 2, 0), 2)
        for t in range(tiles):
            number = c * tiles + t
            first = line_of(first_ref, 2 * number, row) - number * TILE
            own = columns_of(h_refs, 2 * number, 2)
            terms = counted(pair_products(old, own), first) * last_ref[number]
            share += doc_sums(terms, line_of(ids_ref, 2 * number, row))
            old = own
    here = pl.ds(pl.multiple_of(rows_ref[row] * DOCS, DOCS), DOCS)
    acc[here, :] += share

    sums = jnp.sum(acc[...].T, axis=0, keepdims=True)
    out_ref[...] = jnp.broadcast_to(sums[None], out_ref.shape)


def in_vmem(count):
    return [pl.BlockSpec(memory_space=pltpu.VMEM)] * count


def in_hbm(count):
    return [pl.BlockSpec(memory_space=pltpu.HBM)] * count


def keep_in(space, array):
    return pltpu.with_memory_space_constraint(array, space)


def gram_cost(nrows, grad):
    blocks, _, _, width = grad.shape
    return pl.CostEstimate(
        flops=nrows * blocks * BLK * 4 * TILE * (TILE + width),
        bytes_accessed=grad.size * 2,
        transcendentals=0,
    )


def gram_early(rows, ids, kinds, pairs, grad):
    every = grad.shape[1]
    tiles = pairs.shape[1] // PARTS
    return pl.pallas_call(
        functools.partial(early_kernel, kinds),
        out_shape=[
            jax.ShapeDtypeStruct((every * DOCS, BLK), jnp.float32),
            pltpu.VMEM(grad.shape, grad.dtype),
            pltpu.VMEM((pairs.shape[1], TILE, TILE), jnp.float32),
        ],
        grid_spec=pltpu.PrefetchScalarGridSpec(
            num_scalar_prefetch=1,
            grid=(),
            in_specs=[*in_vmem(1), *in_hbm(2)],
            out_specs=in_vmem(3),
            scratch_shapes=[
                pltpu.VMEM((AHEAD + 2, tiles, TILE, TILE), jnp.float32),
                pltpu.SemaphoreType.DMA((len(kinds) * PARTS,)),
                pltpu.SemaphoreType.DMA((every * PARTS,)),
            ],
        ),
        compiler_params=pltpu.CompilerParams(vmem_limit_bytes=12 * 2**20),
        cost_estimate=gram_cost(len(kinds), grad),
        name="gram",
    )(rows, ids, keep_in(pltpu.HBM, pairs), keep_in(pltpu.HBM, grad))


def gram_late(rows, ids, first, row, hidden, last, init, devices):
    return pl.pallas_call(
        functools.partial(late_kernel, row),
        out_shape=jax.ShapeDtypeStruct((devices, 1, BLK), jnp.float32),
        grid_spec=pltpu.PrefetchScalarGridSpec(
            num_scalar_prefetch=1,
            grid=(),
            in_specs=[*in_vmem(2), *in_hbm(len(hidden)), *in_vmem(2)],
            out_specs=pl.BlockSpec(memory_space=pltpu.VMEM),
            scratch_shapes=[
                pltpu.VMEM(init.shape, jnp.float32),
                pltpu.VMEM((len(hidden), *hidden[0].shape), hidden[0].dtype),
                pltpu.SemaphoreType.DMA((PARTS, len(hidden))),
            ],
        ),
        compiler_params=pltpu.CompilerParams(vmem_limit_bytes=8 * 2**20),
        cost_estimate=pl.CostEstimate(
            flops=2 * 2 * last.size * TILE, bytes_accessed=last.size * 4, transcendentals=0
        ),
        name="gram_late",
    )(rows, ids, first, *hidden, keep_in(pltpu.VMEM, last), init)


def product_kernel(nrows, bound, rows_ref, ids_ref, norms_ref, *refs):
    pieces = refs[: HALVES * nrows]
    g_ref, out_ref, h_ref, h_sems, factor, scaled = refs[HALVES * nrows :]
    blocks = g_ref.shape[0]
    steps = blocks // DEPTH

    order = [nrows - 2, *range(nrows - 2), nrows - 1]

    def hidden_copies(k):
        return [
            pltpu.make_async_copy(pieces[n], h_ref.at[n], h_sems.at[n])
            for n in range(HALVES * k, HALVES * (k + 1))
        ]

    for piece in hidden_copies(order[0]):
        piece.start()
    norms = jnp.maximum(jnp.sum(norms_ref[...], axis=0), 0.0)
    clip = bound / jnp.maximum(jnp.sqrt(norms), bound) / nrows
    for k in range(nrows):
        ids = ids_ref[:, k, :] + rows_ref[k] * DOCS
        table = jnp.broadcast_to(clip, ids.shape)
        factor[k] = jnp.take_along_axis(table, ids, axis=1)

    def scale(n, slot):
        k, begin = order[n // steps], n % steps * DEPTH
        lines = jnp.concatenate([factor[k, begin : begin + DEPTH, :]] * (BLK // DEPTH), axis=0).T
        for j in range(DEPTH):
            factors = jnp.broadcast_to(lines[:, j : j + 1], (BLK, BLK))
            for c in range(0, g_ref.shape[3], BLK):
                grad = g_ref[begin + j, k, :, c : c + BLK].astype(jnp.float32)
                scaled[slot, j * BLK : (j + 1) * BLK, c : c + BLK] = (grad * factors).astype(jnp.bfloat16)

    scale(0, 0)
    for n in range(nrows * steps):
        k, begin = order[n // steps], n % steps * DEPTH
        if begin == 0:
            for piece in hidden_copies(k):
                piece.wait()
            if n // steps + 1 < nrows:
                for piece in hidden_copies(order[n // steps + 1]):
                    piece.start()
        if n + 1 < nrows * steps:
            scale(n + 1, (n + 1) % 2)
        share = lax.dot_general(
            columns_of([h_ref.at[HALVES * k + q] for q in range(HALVES)], begin, DEPTH),
            scaled[n % 2],
            TN,
            preferred_element_type=jnp.float32,
        )
        if n == 0:
            out_ref[...] = share
        else:
            out_ref[...] += share


def product(rows, ids, norms, hidden, grad, bound):
    blocks, nrows, _, width = grad.shape
    pieces = [piece for row in hidden for piece in row]
    return pl.pallas_call(
        functools.partial(product_kernel, nrows, bound),
        out_shape=pltpu.HBM((TILE, width), jnp.float32),
        grid_spec=pltpu.PrefetchScalarGridSpec(
            num_scalar_prefetch=1,
            grid=(),
            in_specs=[*in_vmem(2), *in_hbm(len(pieces)), *in_vmem(1)],
            out_specs=pl.BlockSpec(memory_space=pltpu.VMEM),
            scratch_shapes=[
                pltpu.VMEM((len(pieces), *pieces[0].shape), grad.dtype),
                pltpu.SemaphoreType.DMA((len(pieces),)),
                pltpu.VMEM((nrows, blocks, BLK), jnp.float32),
                pltpu.VMEM((2, DEPTH * BLK, width), jnp.bfloat16),
            ],
        ),
        compiler_params=pltpu.CompilerParams(vmem_limit_bytes=14 * 2**20),
        cost_estimate=pl.CostEstimate(
            flops=2 * nrows * blocks * BLK * TILE * width,
            bytes_accessed=nrows * blocks * BLK * 2 * (TILE + width),
            transcendentals=0,
        ),
        name="product",
    )(rows, ids, norms, *pieces, keep_in(pltpu.VMEM, grad))


def quarters_kernel(offsets, me_ref, ids_hbm, grad_ref, *refs):
    *out_refs, ids_ref, sems = refs
    tokens = grad_ref.shape[0]
    part = out_refs[0].shape[1]
    count = len(offsets)
    ids_copy = pltpu.make_async_copy(ids_hbm, ids_ref, sems.at[count])
    ids_copy.start()
    copies = []
    for n, (offset, out_ref) in enumerate(zip(offsets, out_refs)):
        begin = pl.multiple_of(lax.rem(me_ref[0] + offset, count) * part, BLK)
        source = grad_ref.at[:, pl.ds(begin, part)]
        copies.append(pltpu.make_async_copy(source, out_ref.at[pl.ds(0, tokens)], sems.at[n]))
    for copy in copies:
        copy.start()
    ids_copy.wait()
    ids = jnp.broadcast_to(ids_ref[...].astype(jnp.float32).astype(jnp.bfloat16), (16, BLK))
    for out_ref in out_refs:
        out_ref[tokens:, :BLK] = ids
        out_ref[tokens:, BLK:] = jnp.zeros((16, part - BLK), jnp.bfloat16)
    for copy in copies:
        copy.wait()


def quarters(me, offsets, grad, ids):
    tokens, width = grad.shape
    count = len(offsets)
    return pl.pallas_call(
        functools.partial(quarters_kernel, offsets),
        out_shape=[pltpu.VMEM((tokens + 16, width // count), grad.dtype)] * count,
        grid_spec=pltpu.PrefetchScalarGridSpec(
            num_scalar_prefetch=1,
            grid=(),
            in_specs=in_hbm(2),
            out_specs=in_vmem(count),
            scratch_shapes=[
                pltpu.VMEM(ids.shape, ids.dtype),
                pltpu.SemaphoreType.DMA((count + 1,)),
            ],
        ),
        name="quarters",
    )(me, keep_in(pltpu.HBM, ids), keep_in(pltpu.HBM, grad))


def columns_kernel(in_ref, *out_refs):
    for j in range(out_refs[0].shape[0]):
        for q, out_ref in enumerate(out_refs):
            at = (j * HALVES + q) * BLK
            out_ref[j] = in_ref[:, at : at + BLK]


def columns(hidden, blocks, steps=4):
    tokens, width = hidden.shape
    count = blocks // steps
    return pl.pallas_call(
        columns_kernel,
        out_shape=[jax.ShapeDtypeStruct((blocks, tokens, BLK), hidden.dtype)] * HALVES,
        grid=(steps,),
        in_specs=[pl.BlockSpec((tokens, width // steps), lambda i: (0, i))],
        out_specs=[pl.BlockSpec((count, tokens, BLK), lambda i: (i, 0, 0))] * HALVES,
        name="columns",
    )(hidden)


def shift(block, distance):
    size = lax.axis_size("dp")
    return lax.ppermute(block, "dp", [(i, (i + distance) % size) for i in range(size)])


def starts(ids):
    docs = jnp.arange(DOCS, dtype=jnp.int32)
    before = jnp.sum((ids[None] < docs[:, None, None, None]).astype(jnp.int32), axis=(1, 3))
    own = ids[None] == docs[:, None, None, None]
    return jnp.sum(jnp.where(own, before[:, None, :, None], 0), axis=0)


def body(hidden, grad_out, segment):
    row_count = lax.axis_size("dp")
    blocks = lax.axis_size("ctx")
    tokens, width_hidden = hidden.shape[1:]
    width_grad = grad_out.shape[2]
    me = lax.axis_index("dp")

    keep, up, down, across = quarters(me[None], (0, 1, 3, 2), grad_out[0], segment)
    received = [shift(up, 1), shift(down, -1), keep, shift(across, 2)]

    chunks = columns(hidden[0], blocks)
    def rest(received, chunks):
        received, _ = lax.optimization_barrier((received, chunks))

        every_grad = jnp.stack([part[:tokens] for part in received])
        every_grad = lax.all_gather(every_grad, "ctx", axis=0, tiled=False)

        hidden_rows = [[], [], [], []]
        ready = None
        for q, chunk in enumerate(chunks):
            if ready is not None:
                chunk, ready = lax.optimization_barrier((chunk, ready))
            own = lax.all_to_all(chunk, "ctx", 0, 0, tiled=True)
            ready = own
            below, above = lax.optimization_barrier((shift(own, 1), shift(own, -1)))
            far = shift(below, 1) if q < HALVES // 2 else shift(above, -1)
            for row, piece in zip(hidden_rows, (below, above, own, far)):
                row.append(piece)

        ids = jnp.stack([part[tokens, :BLK] for part in received]).astype(jnp.int32)
        ids, ready = lax.optimization_barrier((ids, ready))
        ids = jnp.broadcast_to(ids[None], (blocks, row_count, tokens))
        ids = lax.all_to_all(ids, "ctx", 0, 0, tiled=True)
        first = starts(ids)

        rows = lax.rem(me + jnp.array([3, 1, 0, 2], jnp.int32), row_count)
        kinds = (0, 1, 2)
        pairs = hidden_gram(first, kinds[2:], hidden_rows[2:3], len(kinds))
        pairs = hidden_gram(first, kinds[:2], hidden_rows[:2], len(kinds), pairs)
        early, grads, last = gram_early(rows, ids, kinds, pairs, every_grad)
        devices = row_count * blocks
        partial = gram_late(rows, ids, first, 3, hidden_rows[3], last, early, devices)
        norms = lax.all_to_all(partial, ("dp", "ctx"), 0, 0, tiled=True)

        bound = math.sqrt(tokens * width_hidden * width_grad)
        return product(rows, ids, norms, hidden_rows, grads, bound)

    nothing = lambda *_: jnp.zeros((TILE, width_grad // row_count), jnp.float32)
    return lax.cond(me < row_count, rest, nothing, received, chunks)


def solution(mesh):
    in_specs = (P("dp", "ctx", None), P("dp", "ctx", None), P("dp", "ctx"))
    out_specs = P("ctx", "dp")
    return jax.shard_map(body, mesh=mesh, in_specs=in_specs, out_specs=out_specs, check_vma=False)
```
